256 devices in a mesh: dp: 8 (over y, core), graph: 32 (over x, z).
Axes of the slice: x: 4, y: 4, z: 8, core: 2. Of those that a mesh axis runs over, the one named last changes fastest.
Arguments:
- node_latents: bfloat16 [8, 4096, 512], P('dp', 'graph'), may hold values from -6 to 6
- edge_latents: bfloat16 [8, 256, 128, 512], P('dp', 'graph'), may hold values from -6 to 6
- senders: int32 [256, 128], P('graph'), may hold values from 0 to 4095, as said below
- receivers: int32 [256, 128], P('graph'), may hold values from 0 to 4095, as said below
- block_counts: int32 [32], P('graph'), may hold values from 1 to 8, 128 in all
- edge_first: bfloat16 [3, 512, 512], replicated, may hold values from -0.25 to 0.25
- edge_second: bfloat16 [512, 512], replicated, may hold values from -0.25 to 0.25
- node_first: bfloat16 [2, 512, 512], replicated, may hold values from -0.25 to 0.25
- node_second: bfloat16 [512, 512], replicated, may hold values from -0.25 to 0.25
- vectors: float32 [4, 512], replicated, may hold values from 0.1 to 1.9
- node_cotangent: bfloat16 [8, 4096, 512], P('dp', 'graph'), may hold values from -6 to 6
- edge_cotangent: bfloat16 [8, 256, 128, 512], P('dp', 'graph'), may hold values from -6 to 6
Outputs:
- new_nodes: bfloat16 [8, 4096, 512], P('dp', 'graph')
- new_edges: bfloat16 [8, 256, 128, 512], P('dp', 'graph')
- node_grad: bfloat16 [8, 4096, 512], P('dp', 'graph')
- edge_grad: bfloat16 [8, 256, 128, 512], P('dp', 'graph')
- grad_edge_first: float32 [3, 512, 512], P(None, 'graph')
- grad_edge_second: float32 [512, 512], P('graph')
- grad_node_first: float32 [2, 512, 512], P(None, 'graph')
- grad_node_second: float32 [512, 512], P('graph')
- grad_vectors: float32 [4, 512], P(None, 'graph')
The draws below stay inside these ranges and needn't reach their ends.
Inputs may be any that keep to these rules, and one draw needn't show every extreme that they name: `senders`: exactly 8 * 128 // 32 of the edges of blocks d * 8 to d * 8 + 7 have their sender among nodes o * 128 to o * 128 + 127, for every d and o (a sender node may repeat). Edges of block b have receivers among nodes (b // 8) * 128 to (b // 8) * 128 + 127. `block_counts`: the counts sum to 128; some device has all 8 blocks live.
All inputs are finite; a program needn't handle non-finite values.
Results may differ from the reference program's by a relative error of at most 0.027.
Values may be sent and summed in bfloat16 or wider, within the bound.
A program may use at most 128 MiB of HBM per device.

```python
import math
import jax
import jax.numpy as jnp
import numpy as np
from jax import lax

D = 512
NODE_DEV = 128
EB = 8
BLOCK = 128
NODES = 4096
BLOCKS = 256
N_DP = 8
N_GRAPH = 32


def draw_receivers(key, part):
    key = jax.random.fold_in(key, 7)
    within = jax.random.randint(key, (BLOCKS, BLOCK), 0, NODE_DEV)
    owner = jnp.arange(BLOCKS, dtype=jnp.int32) // EB * NODE_DEV
    return (within + owner[:, None]).astype(jnp.int32)


def draw_senders(key, part):
    key = jax.random.fold_in(key, 11)
    per_owner = EB * BLOCK // N_GRAPH
    base = jnp.repeat(jnp.arange(N_GRAPH, dtype=jnp.int32), per_owner)
    keys = jax.random.split(key, N_GRAPH + 1)
    owners = jax.vmap(lambda single: jax.random.permutation(single, base))(keys[:N_GRAPH])
    within = jax.random.randint(keys[N_GRAPH], (N_GRAPH, EB * BLOCK), 0, NODE_DEV)
    return (owners * NODE_DEV + within).reshape(BLOCKS, BLOCK).astype(jnp.int32)


def level_of(stream_key, shape, shards, low, high):
    def one(dim, shards_of):
        heights = jax.random.uniform(jax.random.fold_in(jax.random.fold_in(stream_key, 6), dim), (shards_of,), jnp.float32, low / len(shards), high / len(shards))
        return jnp.repeat(jnp.exp(heights), shape[dim] // shards_of).reshape((-1,) + (1,) * (len(shape) - dim - 1))

    loudness = one(*shards[0])
    for cut in shards[1:]:
        loudness = loudness * one(*cut)
    return loudness


def split_up(amount, total, most, slope):
    weights = [(1 << 20) // math.isqrt(rank ** slope) + 1 for rank in range(2, amount + 1)]
    spare, holding = total - most - (amount - 1), [1] * (amount - 1)
    while spare > 0:
        free = [i for i in range(amount - 1) if holding[i] < most]
        pool, budget = sum([weights[i] for i in free]), spare
        for i in free:
            extra = min(most - holding[i], max(1, budget * weights[i] // pool), spare)
            holding[i] = holding[i] + extra
            spare = spare - extra
    return np.array([most] + holding)


def uneven(key, count, total, most, lean):
    if count == 2:
        one = jax.random.randint(key, (), max(1, total - most), min(most, total - 1) + 1)
        return jnp.stack([one, total - one])
    lengths = jnp.asarray(split_up(count, total, most, lean), jnp.int32)
    twos = (count - 1) // 2
    donor, sink = lengths[1:1 + 2 * twos:2], lengths[2:2 + 2 * twos:2]
    room = jnp.minimum(donor - 1, most - sink)
    moved = jax.random.randint(jax.random.fold_in(key, 1), (twos,), 0, 1 << 20) % (room + 1)
    lengths = lengths.at[1:1 + 2 * twos:2].set(donor - moved).at[2:2 + 2 * twos:2].set(sink + moved)
    return lengths[jax.random.permutation(jax.random.fold_in(key, 2), count)]


def noise(rng, extent, scale, limit, pieces=(), held_as=jnp.bfloat16):
    gain = level_of(rng, extent, pieces, -0.22, 0.18) if pieces else 1.0
    values = jax.random.normal(rng, extent, jnp.float32) * scale * gain
    return jnp.minimum(jnp.maximum(values, -limit), limit).astype(held_as)


def setup_inputs(seed: int = 0) -> dict:
    splits = jax.random.split(jax.random.key(seed), 13)
    return {
        "node_latents": noise(splits[0], (N_DP, NODES, D), 1.0, 6.0, ((0, 8), (1, 32))),
        "edge_latents": noise(splits[1], (N_DP, BLOCKS, BLOCK, D), 1.0, 6.0, ((0, 8), (1, 32))),
        "senders": draw_senders(jax.random.fold_in(splits[12], 71), 0),
        "receivers": draw_receivers(jax.random.fold_in(splits[12], 71), 0),
        "block_counts": uneven(splits[4], N_GRAPH, N_GRAPH * EB // 2, EB, 2).astype(jnp.int32),
        "edge_first": noise(splits[5], (3, D, D), D ** -0.5, 0.25),
        "edge_second": noise(splits[6], (D, D), D ** -0.5, 0.25),
        "node_first": noise(splits[7], (2, D, D), D ** -0.5, 0.25),
        "node_second": noise(splits[8], (D, D), D ** -0.5, 0.25),
        "vectors": jnp.clip(1.0 + 0.18 * jax.random.normal(splits[9], (4, D), jnp.float32), 0.1, 1.9),
        "node_cotangent": noise(splits[10], (N_DP, NODES, D), 1.0, 6.0, ((0, 8), (1, 32))),
        "edge_cotangent": noise(splits[11], (N_DP, BLOCKS, BLOCK, D), 1.0, 6.0, ((0, 8), (1, 32))),
    }


EPSILON = 1e-05

def product(left, right):
    return jnp.dot(left, right, preferred_element_type=jnp.float32)

def product_back(left, right):
    return lax.dot_general(left, right, (((1,), (1,)), ((), ())), preferred_element_type=jnp.float32)

def product_over(left, right):
    return lax.dot_general(left, right, (((0,), (0,)), ((), ())), preferred_element_type=jnp.float32)

def norm_forward(values, scales):
    average = lax.optimization_barrier(jnp.mean(values, -1, keepdims=True))
    centered = values - average
    inverse = lax.rsqrt(lax.optimization_barrier(jnp.mean(centered * centered, -1, keepdims=True)) + EPSILON)
    normed = centered * inverse
    return (normed * scales, normed, inverse)

def norm_backward(upstream, normed, inverse, scales):
    scaled = upstream * scales
    return inverse * (scaled - lax.optimization_barrier(jnp.mean(scaled, -1, keepdims=True)) - normed * lax.optimization_barrier(jnp.mean(scaled * normed, -1, keepdims=True)))

def silu_slope(values):
    sigmoid = jax.nn.sigmoid(values)
    return sigmoid * (1.0 + values * (1.0 - sigmoid))

def reference(node_latents, edge_latents, senders, receivers, block_counts, edge_first, edge_second, node_first, node_second, vectors, node_cotangent, edge_cotangent):
    block_index = jnp.arange(BLOCKS, dtype=jnp.int32)
    live_blocks = (block_index % EB < block_counts[block_index // EB]).astype(jnp.float32)
    live_rows = jnp.broadcast_to(live_blocks[:, None], (BLOCKS, BLOCK)).reshape(-1, 1)
    send_index = senders.reshape(-1)
    recv_index = receivers.reshape(-1)

    def one_state(inputs):
        node_rows, edge_block, node_cot, edge_cot = inputs
        flat_edges = edge_block.reshape(BLOCKS * BLOCK, D)
        flat_cot = edge_cot.reshape(BLOCKS * BLOCK, D).astype(jnp.float32)
        sent_rows = node_rows[send_index]
        recv_rows = node_rows[recv_index]
        edge_pre = product(flat_edges, edge_first[0]) + product(sent_rows, edge_first[1]) + product(recv_rows, edge_first[2]) + vectors[0]
        edge_act = jax.nn.silu(edge_pre).astype(jnp.bfloat16)
        message, edge_normed, edge_inverse = norm_forward(product(edge_act, edge_second), vectors[2])
        message_b = (live_rows * message).astype(jnp.bfloat16)
        new_edges = (flat_edges.astype(jnp.float32) + message_b.astype(jnp.float32)).astype(jnp.bfloat16)
        aggregate = jax.ops.segment_sum(message_b.astype(jnp.float32), recv_index, num_segments=NODES).astype(jnp.bfloat16)
        node_pre = product(node_rows, node_first[0]) + product(aggregate, node_first[1]) + vectors[1]
        node_act = jax.nn.silu(node_pre).astype(jnp.bfloat16)
        node_out, node_normed, node_inverse = norm_forward(product(node_act, node_second), vectors[3])
        new_nodes = (node_rows.astype(jnp.float32) + node_out).astype(jnp.bfloat16)
        upstream = node_cot.astype(jnp.float32)
        node_dz = norm_backward(upstream, node_normed, node_inverse, vectors[3]).astype(jnp.bfloat16)
        node_dpre = (product_back(node_dz, node_second) * silu_slope(node_pre)).astype(jnp.bfloat16)
        aggregate_cot = product_back(node_dpre, node_first[1]).astype(jnp.bfloat16)
        message_cot = live_rows * (flat_cot + aggregate_cot[recv_index].astype(jnp.float32))
        edge_dz = norm_backward(message_cot, edge_normed, edge_inverse, vectors[2]).astype(jnp.bfloat16)
        edge_dpre = (product_back(edge_dz, edge_second) * silu_slope(edge_pre)).astype(jnp.bfloat16)
        edge_grad = (flat_cot + product_back(edge_dpre, edge_first[0])).astype(jnp.bfloat16)
        from_send = jax.ops.segment_sum(product_back(edge_dpre, edge_first[1]), send_index, num_segments=NODES)
        from_recv = jax.ops.segment_sum(product_back(edge_dpre, edge_first[2]), recv_index, num_segments=NODES)
        node_grad = (upstream + product_back(node_dpre, node_first[0]) + from_send + from_recv).astype(jnp.bfloat16)
        matrices = jnp.stack([product_over(flat_edges, edge_dpre), product_over(sent_rows, edge_dpre), product_over(recv_rows, edge_dpre), product_over(edge_act, edge_dz), product_over(node_rows, node_dpre), product_over(aggregate, node_dpre), product_over(node_act, node_dz)])
        columns = jnp.stack([lax.optimization_barrier(jnp.sum(edge_dpre.astype(jnp.float32), 0)), lax.optimization_barrier(jnp.sum(node_dpre.astype(jnp.float32), 0)), lax.optimization_barrier(jnp.sum(message_cot * edge_normed, 0)), lax.optimization_barrier(jnp.sum(upstream * node_normed, 0))])
        return (new_nodes, new_edges.reshape(BLOCKS, BLOCK, D), node_grad, edge_grad.reshape(BLOCKS, BLOCK, D), matrices, columns)
    new_nodes, new_edges, node_grad, edge_grad, matrices, columns = lax.map(one_state, (node_latents, edge_latents, node_cotangent, edge_cotangent))
    matrices = lax.optimization_barrier(jnp.sum(matrices, 0))
    columns = lax.optimization_barrier(jnp.sum(columns, 0))
    return (new_nodes, new_edges, node_grad, edge_grad, matrices[0:3], matrices[3], matrices[4:6], matrices[6], columns)
```

```python
import jax
import jax.numpy as jnp
from jax import lax
from jax.experimental import pallas as pl
from jax.experimental.pallas import tpu as pltpu
from jax.sharding import PartitionSpec as P

EPSILON = 1e-05
MESH = pl.DeviceIdType.MESH
F32 = jnp.float32
BF16 = jnp.bfloat16

XN, ZN, YN = 4, 8, 4
GN = XN * ZN
ND = 128
D = 512
EDGES = 1024
SLOTS = 32
BM = 256
NB = EDGES // BM
VMEM_LIMIT = 56 * 1024 * 1024

RING_ORDER = (0, 1, 5, 2, 6, 3, 7, 4)
RING_OFFSET = (0, -1, -2, -3, -4, 1, 2, 3)


def nn(left, right):
    return jnp.dot(left, right, preferred_element_type=F32)


def nt(left, right):
    return lax.dot_general(left, right, (((1,), (1,)), ((), ())), preferred_element_type=F32)


def tn(left, right):
    return lax.dot_general(left, right, (((0,), (0,)), ((), ())), preferred_element_type=F32)


def place():
    dp = lax.axis_index("dp")
    graph = lax.axis_index("graph")
    return dp, graph // ZN, graph % ZN


def remote(src, dst, send, recv, device):
    return pltpu.make_async_remote_copy(
        src_ref=src, dst_ref=dst, send_sem=send, recv_sem=recv, device_id=device, device_id_type=MESH
    )


def enter(devices):
    barrier = pltpu.get_barrier_semaphore()
    for device in devices:
        pl.semaphore_signal(barrier, inc=1, device_id=device, device_id_type=MESH)
    pl.semaphore_wait(barrier, len(devices))


def onehot_rows(count, row):
    index = lax.broadcasted_iota(jnp.int32, (count, row.shape[1]), 0)
    return jnp.where(index == row, 1.0, 0.0).astype(BF16)


def exchange_kernel(
    node_ref,
    senders_ref,
    buf_ref,
    slot_ref,
    list_ref,
    ring,
    lists_own,
    lists_in,
    stage,
    ring_send,
    ring_recv,
    list_send,
    list_recv,
    x_send,
    x_recv,
):
    dp, x, z = place()
    up = (dp, x * ZN + (z + 1) % ZN)
    down = (dp, x * ZN + (z + ZN - 1) % ZN)
    peers = [None] + [(dp, ((x + k) % XN) * ZN + z) for k in range(1, XN)]
    enter([up, down] + peers[1:])

    def hop(src, slot, device):
        copy = remote(src, ring.at[slot], ring_send.at[slot], ring_recv.at[slot], device)
        copy.start()
        return copy

    hops = {1: hop(node_ref, 1, up), 5: hop(node_ref, 5, down)}

    senders = senders_ref[...]
    owners = senders // ND
    local = (senders % ND).astype(F32)
    earlier = jnp.where(
        lax.broadcasted_iota(jnp.int32, (ND, ND), 0) < lax.broadcasted_iota(jnp.int32, (ND, ND), 1), 1.0, 0.0
    ).astype(BF16)
    base = jnp.zeros((GN, 1), F32)
    table = jnp.zeros((GN, ND), F32)
    lane = lax.broadcasted_iota(jnp.int32, (ND, ND), 0)
    group = lax.broadcasted_iota(jnp.int32, (GN, ND), 0)
    for b in range(EDGES // ND):
        owner = owners[b : b + 1, :]
        mine = jnp.where(group == owner, 1.0, 0.0)
        before = nn(mine.astype(BF16), earlier) + base
        rank = jnp.sum(mine * before, axis=0, keepdims=True).astype(jnp.int32)
        base = base + jnp.sum(mine, axis=1, keepdims=True)
        slot_ref[b : b + 1, :] = owner * SLOTS + rank
        column = jnp.where(lane == rank + SLOTS * x, 1.0, 0.0).astype(BF16)
        table = table + nt((mine * local[b : b + 1, :]).astype(BF16), column)
    lists_own[...] = table.reshape(XN, ZN, ND)

    list_copies = []
    for k in range(1, XN):
        copy = remote(lists_own.at[(x + k) % XN], lists_in.at[k - 1], list_send.at[k - 1], list_recv.at[k - 1], peers[k])
        copy.start()
        list_copies.append(copy)
    for copy in list_copies:
        copy.wait_recv()
    list_ref[...] = (lists_own[x] + lists_in[0] + lists_in[1] + lists_in[2]).astype(jnp.int32)

    x_copies = []
    for place_of in RING_ORDER:
        source = (z + RING_OFFSET[place_of] + ZN) % ZN
        if place_of:
            hops[place_of].wait_recv()
            if place_of in (1, 2, 3):
                hops[place_of + 1] = hop(ring.at[place_of], place_of + 1, up)
            elif place_of in (5, 6):
                hops[place_of + 1] = hop(ring.at[place_of], place_of + 1, down)
            block = ring[place_of]
        else:
            block = node_ref[...]
        chosen = onehot_rows(ND, list_ref[pl.ds(source, 1), :])
        stage[place_of] = tn(chosen, block).astype(BF16).reshape(XN, SLOTS, D)
        buf_ref[x * ZN + source] = stage[place_of, x]
        for k in range(1, XN):
            copy = remote(
                stage.at[place_of, (x + k) % XN],
                buf_ref.at[x * ZN + source],
                x_send.at[place_of, k - 1],
                x_recv.at[place_of, k - 1],
                peers[k],
            )
            copy.start()
            x_copies.append(copy)
    for copy in x_copies:
        copy.wait_recv()
    for copy in list_copies + list(hops.values()) + x_copies:
        copy.wait_send()


def exchange(node_rows, senders):
    vmem = pl.BlockSpec(memory_space=pltpu.VMEM)
    return pl.pallas_call(
        exchange_kernel,
        out_shape=(
            jax.ShapeDtypeStruct((GN, SLOTS, D), BF16),
            jax.ShapeDtypeStruct((EDGES // ND, ND), jnp.int32),
            jax.ShapeDtypeStruct((ZN, ND), jnp.int32),
        ),
        in_specs=[vmem] * 2,
        out_specs=(vmem,) * 3,
        scratch_shapes=[
            pltpu.VMEM((ZN, ND, D), BF16),
            pltpu.VMEM((XN, ZN, ND), F32),
            pltpu.VMEM((XN - 1, ZN, ND), F32),
            pltpu.VMEM((ZN, XN, SLOTS, D), BF16),
            pltpu.SemaphoreType.DMA((ZN,)),
            pltpu.SemaphoreType.DMA((ZN,)),
            pltpu.SemaphoreType.DMA((XN - 1,)),
            pltpu.SemaphoreType.DMA((XN - 1,)),
            pltpu.SemaphoreType.DMA((ZN, XN - 1)),
            pltpu.SemaphoreType.DMA((ZN, XN - 1)),
        ],
        compiler_params=pltpu.CompilerParams(
            collective_id=0, has_side_effects=True, vmem_limit_bytes=VMEM_LIMIT
        ),
        name="exchange",
    )(node_rows, senders)


def normalize(values):
    average = jnp.mean(values, -1, keepdims=True)
    centered = values - average
    inverse = lax.rsqrt(jnp.mean(centered * centered, -1, keepdims=True) + EPSILON)
    return centered * inverse, inverse


def norm_backward(upstream, normed, inverse, scales):
    scaled = upstream * scales
    return inverse * (
        scaled
        - jnp.mean(scaled, -1, keepdims=True)
        - normed * jnp.mean(scaled * normed, -1, keepdims=True)
    )


def sigmoid(values):
    return 0.5 + 0.5 * jnp.tanh(0.5 * values)


def dense_kernel(
    counts_ref,
    node_ref,
    edge_ref,
    buf_ref,
    slot_ref,
    recv_ref,
    edge_first_ref,
    edge_second_ref,
    node_first_ref,
    node_second_ref,
    vectors_ref,
    node_cot_ref,
    edge_cot_ref,
    new_nodes_ref,
    new_edges_ref,
    edge_grad_ref,
    node_part_ref,
    back_ref,
    grads_ref,
    perm,
    recv_hot,
    act,
    slope,
    normed,
    inverse,
    dz,
    dpre,
):
    first_node = lax.axis_index("graph") * ND
    live_rows = counts_ref[0] * 128
    h = node_ref[...]
    h_recv = nn(h, edge_first_ref[2]).astype(BF16)
    aggregate = jnp.zeros((ND, D), F32)
    per = BM // 128
    for i in range(NB):
        rows = slice(i * BM, (i + 1) * BM)
        slot = jnp.concatenate([slot_ref[i * per + j : i * per + j + 1, :] for j in range(per)], axis=1)
        recv = jnp.concatenate([recv_ref[i * per + j : i * per + j + 1, :] for j in range(per)], axis=1)
        perm[:, rows] = onehot_rows(EDGES, slot)
        recv_hot[:, rows] = onehot_rows(ND, recv - first_node)
        sent = tn(perm[:, rows], buf_ref[...]).astype(BF16)
        e = edge_ref[rows, :]
        pre = (
            nn(e, edge_first_ref[0])
            + nn(sent, edge_first_ref[1])
            + tn(recv_hot[:, rows], h_recv)
            + vectors_ref[0:1, :]
        )
        gate = sigmoid(pre)
        act_b = (pre * gate).astype(BF16)
        act[rows, :] = act_b
        slope[rows, :] = gate * (1.0 + pre * (1.0 - gate))
        hat, inv = normalize(nn(act_b, edge_second_ref[...]))
        normed[rows, :] = hat
        inverse[rows, :] = inv
        live = lax.broadcasted_iota(jnp.int32, (BM, 1), 0) + i * BM < live_rows
        message = jnp.where(live, hat * vectors_ref[2:3, :], 0.0).astype(BF16)
        new_edges_ref[rows, :] = (e.astype(F32) + message.astype(F32)).astype(BF16)
        aggregate = aggregate + nn(recv_hot[:, rows], message)
    aggregate = aggregate.astype(BF16)

    node_pre = nn(h, node_first_ref[0]) + nn(aggregate, node_first_ref[1]) + vectors_ref[1:2, :]
    node_gate = sigmoid(node_pre)
    node_act = (node_pre * node_gate).astype(BF16)
    node_hat, node_inv = normalize(nn(node_act, node_second_ref[...]))
    new_nodes_ref[...] = (h.astype(F32) + node_hat * vectors_ref[3:4, :]).astype(BF16)
    upstream = node_cot_ref[...].astype(F32)
    node_dz = norm_backward(upstream, node_hat, node_inv, vectors_ref[3:4, :]).astype(BF16)
    node_dpre = (
        nt(node_dz, node_second_ref[...]) * (node_gate * (1.0 + node_pre * (1.0 - node_gate)))
    ).astype(BF16)
    aggregate_cot = nt(node_dpre, node_first_ref[1]).astype(BF16)

    col_edge = jnp.zeros((1, D), F32)
    col_scale = jnp.zeros((1, D), F32)
    received = jnp.zeros((ND, D), F32)
    back = jnp.zeros((EDGES, D), F32)
    for i in range(NB):
        rows = slice(i * BM, (i + 1) * BM)
        live = lax.broadcasted_iota(jnp.int32, (BM, 1), 0) + i * BM < live_rows
        cot = edge_cot_ref[rows, :].astype(F32)
        message_cot = jnp.where(live, cot + tn(recv_hot[:, rows], aggregate_cot), 0.0)
        hat = normed[rows, :]
        col_scale = col_scale + jnp.sum(message_cot * hat, 0, keepdims=True)
        dz_b = norm_backward(message_cot, hat, inverse[rows, :], vectors_ref[2:3, :]).astype(BF16)
        dz[rows, :] = dz_b
        dpre_b = (nt(dz_b, edge_second_ref[...]) * slope[rows, :]).astype(BF16)
        dpre[rows, :] = dpre_b
        col_edge = col_edge + jnp.sum(dpre_b.astype(F32), 0, keepdims=True)
        edge_grad_ref[rows, :] = (cot + nt(dpre_b, edge_first_ref[0])).astype(BF16)
        received = received + nn(recv_hot[:, rows], dpre_b)
    back_ref[...] = nn(perm[...], dpre[...]).astype(BF16)
    received = received.astype(BF16)
    node_part_ref[...] = upstream + nt(node_dpre, node_first_ref[0]) + nt(received, edge_first_ref[2])

    grads_ref[0] = tn(edge_ref[...], dpre[...]).astype(BF16)
    grads_ref[1] = tn(buf_ref[...], back_ref[...]).astype(BF16)
    grads_ref[2] = tn(h, received).astype(BF16)
    grads_ref[3] = tn(act[...], dz[...]).astype(BF16)
    grads_ref[4] = tn(h, node_dpre).astype(BF16)
    grads_ref[5] = tn(aggregate, node_dpre).astype(BF16)
    grads_ref[6] = tn(node_act, node_dz).astype(BF16)
    columns = jnp.concatenate(
        [
            col_edge,
            jnp.sum(node_dpre.astype(F32), 0, keepdims=True),
            col_scale,
            jnp.sum(upstream * node_hat, 0, keepdims=True),
            jnp.zeros((124, D), F32),
        ],
        axis=0,
    )
    grads_ref[7, :, 0:128] = columns.T.astype(BF16)
    grads_ref[7, :, 128:512] = jnp.zeros((D, 384), BF16)


def dense(counts, node, edges, buf, slot, recv, edge_first, edge_second, node_first, node_second, vectors, node_cot, edge_cot):
    vmem = pl.BlockSpec(memory_space=pltpu.VMEM)
    return pl.pallas_call(
        dense_kernel,
        out_shape=(
            jax.ShapeDtypeStruct((ND, D), BF16),
            jax.ShapeDtypeStruct((EDGES, D), BF16),
            jax.ShapeDtypeStruct((EDGES, D), BF16),
            jax.ShapeDtypeStruct((ND, D), F32),
            jax.ShapeDtypeStruct((EDGES, D), BF16),
            jax.ShapeDtypeStruct((8, D, D), BF16),
        ),
        in_specs=[pl.BlockSpec(memory_space=pltpu.SMEM)] + [vmem] * 12,
        out_specs=(vmem,) * 6,
        scratch_shapes=[
            pltpu.VMEM((EDGES, EDGES), BF16),
            pltpu.VMEM((ND, EDGES), BF16),
            pltpu.VMEM((EDGES, D), BF16),
            pltpu.VMEM((EDGES, D), F32),
            pltpu.VMEM((EDGES, D), F32),
            pltpu.VMEM((EDGES, 1), F32),
            pltpu.VMEM((EDGES, D), BF16),
            pltpu.VMEM((EDGES, D), BF16),
        ],
        compiler_params=pltpu.CompilerParams(vmem_limit_bytes=VMEM_LIMIT),
        name="dense",
    )(counts, node, edges, buf, slot, recv, edge_first, edge_second, node_first, node_second, vectors, node_cot, edge_cot)


REDUCE_ORDER = (4, 7, 3, 6, 2, 5, 1, 0)
REDUCE_OFFSET = (0, 1, 2, 3, 4, -1, -2, -3)


def reduce_kernel(
    back_ref,
    list_ref,
    grads_ref,
    node_part_ref,
    weight_ref,
    node_grad_ref,
    edge_first_ref,
    edge_second_ref,
    node_first_ref,
    node_second_ref,
    columns_ref,
    rows_in,
    ring_out,
    ring_in,
    core_in,
    pair,
    y_in,
    y_sum,
    x_in,
    x_sum,
    z_in,
    final,
    back_send,
    back_recv,
    ring_send,
    ring_recv,
    core_send,
    core_recv,
    y_send,
    y_recv,
    x_send,
    x_recv,
    z_send,
    z_recv,
    dp_send,
    dp_recv,
):
    dp, x, z = place()
    graph = x * ZN + z
    y, core = dp // 2, dp % 2
    partner = (y * 2 + (1 - core), graph)
    x_peers = [None] + [(dp, ((x + k) % XN) * ZN + z) for k in range(1, XN)]
    z_peers = [None] + [(dp, x * ZN + (z + k) % ZN) for k in range(1, ZN)]
    y_peers = [None] + [(((y + k) % YN) * 2 + core, graph) for k in range(1, YN)]
    dp_peers = [None] + [((dp + k) % 8, graph) for k in range(1, 8)]
    enter(x_peers[1:] + z_peers[1:] + dp_peers[1:])
    up, down = z_peers[1], z_peers[ZN - 1]
    sent = []

    def start(src, dst, send, recv, device):
        copy = remote(src, dst, send, recv, device)
        copy.start()
        sent.append(copy)
        return copy

    other = (1 - core) * 4
    mine = core * 4
    core_copies = []
    for j in range(YN):
        tile = (y + YN - j) % YN if False else j
        core_copies.append(
            start(
                grads_ref.at[pl.ds(other, 4), :, tile * 128 : (tile + 1) * 128],
                core_in.at[tile],
                core_send.at[tile],
                core_recv.at[tile],
                partner,
            )
        )
    row_copies = {}
    for j in REDUCE_ORDER:
        target = (z + REDUCE_OFFSET[j] + ZN) % ZN
        rows_in[j, x] = back_ref[x * ZN + target]
        row_copies[j] = [
            start(
                back_ref.at[((x + k) % XN) * ZN + target],
                rows_in.at[j, x],
                back_send.at[j, k - 1],
                back_recv.at[j, k - 1],
                x_peers[k],
            )
            for k in range(1, XN)
        ]
    for j in range(YN):
        core_copies[j].wait_recv()
        pair[j] = (
            grads_ref[pl.ds(mine, 4), :, j * 128 : (j + 1) * 128].astype(F32) + core_in[j].astype(F32)
        ).astype(BF16)
    y_copies = [
        start(pair.at[(y + k) % YN], y_in.at[k - 1], y_send.at[k - 1], y_recv.at[k - 1], y_peers[k])
        for k in (2, 1, 3)
    ]

    ring_copies = {}
    for j in REDUCE_ORDER:
        target = (z + REDUCE_OFFSET[j] + ZN) % ZN
        for copy in row_copies[j]:
            copy.wait_recv()
        total = nn(onehot_rows(ND, list_ref[pl.ds(target, 1), :]), rows_in[j].reshape(ND, D))
        if j in (3, 2, 1, 6, 5):
            ring_copies[j + 1].wait_recv()
            total = total + ring_in[j + 1].astype(F32)
        if j == 0:
            ring_copies[1].wait_recv()
            ring_copies[5].wait_recv()
            total = total + ring_in[1].astype(F32) + ring_in[5].astype(F32)
            node_grad_ref[...] = (node_part_ref[...] + nt(total.astype(BF16), weight_ref[1])).astype(BF16)
        else:
            ring_out[j] = total.astype(BF16)
            ring_copies[j] = start(
                ring_out.at[j], ring_in.at[j], ring_send.at[j], ring_recv.at[j], up if j < 5 else down
            )

    for copy in y_copies:
        copy.wait_recv()
    y_sum[...] = (
        pair[y].astype(F32) + y_in[0].astype(F32) + y_in[1].astype(F32) + y_in[2].astype(F32)
    ).astype(BF16)
    x_copies = [
        start(
            y_sum.at[:, pl.ds(pl.multiple_of(((x + k) % XN) * 128, 128), 128), :],
            x_in.at[k - 1],
            x_send.at[k - 1],
            x_recv.at[k - 1],
            x_peers[k],
        )
        for k in (2, 1, 3)
    ]
    for copy in x_copies:
        copy.wait_recv()
    x_sum[...] = (
        y_sum[:, pl.ds(pl.multiple_of(x * 128, 128), 128), :].astype(F32)
        + x_in[0].astype(F32)
        + x_in[1].astype(F32)
        + x_in[2].astype(F32)
    ).astype(BF16)
    z_copies = [
        start(
            x_sum.at[:, pl.ds(pl.multiple_of(((z + k) % ZN) * 16, 16), 16), :],
            z_in.at[k - 1],
            z_send.at[k - 1],
            z_recv.at[k - 1],
            z_peers[k],
        )
        for k in (4, 3, 5, 2, 6, 1, 7)
    ]
    for copy in z_copies:
        copy.wait_recv()
    total = x_sum[:, pl.ds(pl.multiple_of(z * 16, 16), 16), :].astype(F32)
    for k in range(ZN - 1):
        total = total + z_in[k].astype(F32)
    final[dp] = total
    dp_copies = [
        start(final.at[dp], final.at[dp], dp_send.at[k - 1], dp_recv.at[k - 1], dp_peers[k]) for k in range(1, 8)
    ]
    for copy in dp_copies:
        copy.wait_recv()
    for j in range(YN):
        lanes = slice(j * 128, (j + 1) * 128)
        for m in range(3):
            edge_first_ref[m, :, lanes] = final[2 * j, m]
        edge_second_ref[:, lanes] = final[2 * j, 3]
        for m in range(2):
            node_first_ref[m, :, lanes] = final[2 * j + 1, m]
        node_second_ref[:, lanes] = final[2 * j + 1, 2]
    columns_ref[...] = final[1, 3]
    for copy in sent:
        copy.wait_send()


def reduce(back, lists, grads, node_part, weight):
    vmem = pl.BlockSpec(memory_space=pltpu.VMEM)
    dma = pltpu.SemaphoreType.DMA
    return pl.pallas_call(
        reduce_kernel,
        out_shape=(
            jax.ShapeDtypeStruct((ND, D), BF16),
            jax.ShapeDtypeStruct((3, 16, D), F32),
            jax.ShapeDtypeStruct((16, D), F32),
            jax.ShapeDtypeStruct((2, 16, D), F32),
            jax.ShapeDtypeStruct((16, D), F32),
            jax.ShapeDtypeStruct((16, 128), F32),
        ),
        in_specs=[vmem] * 5,
        out_specs=(vmem,) * 6,
        scratch_shapes=[
            pltpu.VMEM((ZN, XN, SLOTS, D), BF16),
            pltpu.VMEM((ZN, ND, D), BF16),
            pltpu.VMEM((ZN, ND, D), BF16),
            pltpu.VMEM((YN, 4, D, 128), BF16),
            pltpu.VMEM((YN, 4, D, 128), BF16),
            pltpu.VMEM((YN - 1, 4, D, 128), BF16),
            pltpu.VMEM((4, D, 128), BF16),
            pltpu.VMEM((XN - 1, 4, 128, 128), BF16),
            pltpu.VMEM((4, 128, 128), BF16),
            pltpu.VMEM((ZN - 1, 4, 16, 128), BF16),
            pltpu.VMEM((8, 4, 16, 128), F32),
            dma((ZN, XN - 1)),
            dma((ZN, XN - 1)),
            dma((ZN,)),
            dma((ZN,)),
            dma((YN,)),
            dma((YN,)),
            dma((YN - 1,)),
            dma((YN - 1,)),
            dma((XN - 1,)),
            dma((XN - 1,)),
            dma((ZN - 1,)),
            dma((ZN - 1,)),
            dma((7,)),
            dma((7,)),
        ],
        compiler_params=pltpu.CompilerParams(
            collective_id=1, has_side_effects=True, vmem_limit_bytes=VMEM_LIMIT
        ),
        name="reduce",
    )(back, lists, grads, node_part, weight)


def body(
    node_latents,
    edge_latents,
    senders,
    receivers,
    block_counts,
    edge_first,
    edge_second,
    node_first,
    node_second,
    vectors,
    node_cotangent,
    edge_cotangent,
):
    node = node_latents[0]
    buf, slot, lists = exchange(node, senders)
    new_nodes, new_edges, edge_grad, node_part, back, grads = dense(
        block_counts,
        node,
        edge_latents.reshape(EDGES, D),
        buf.reshape(EDGES, D),
        slot,
        receivers,
        edge_first,
        edge_second,
        node_first,
        node_second,
        vectors,
        node_cotangent[0],
        edge_cotangent.reshape(EDGES, D),
    )
    node_grad, grad_ef, grad_es, grad_nf, grad_ns, columns = reduce(
        back.reshape(GN, SLOTS, D), lists, grads, node_part, edge_first
    )
    shape = edge_latents.shape
    return (
        new_nodes[None],
        new_edges.reshape(shape),
        node_grad[None],
        edge_grad.reshape(shape),
        grad_ef,
        grad_es,
        grad_nf,
        grad_ns,
        columns[:, 0:4].T,
    )


def solution(mesh):
    return jax.shard_map(
        body,
        mesh=mesh,
        in_specs=(
            P("dp", "graph", None),
            P("dp", "graph", None, None),
            P("graph", None),
            P("graph", None),
            P("graph"),
            P(),
            P(),
            P(),
            P(),
            P(),
            P("dp", "graph", None),
            P("dp", "graph", None, None),
        ),
        out_specs=(
            P("dp", "graph", None),
            P("dp", "graph", None, None),
            P("dp", "graph", None),
            P("dp", "graph", None, None),
            P(None, "graph", None),
            P("graph", None),
            P(None, "graph", None),
            P("graph", None),
            P(None, "graph"),
        ),
        check_vma=False,
    )
```

```python
from types import SimpleNamespace

import jax
import jax.numpy as jnp
from jax import lax
from jax.experimental import pallas as pl
from jax.experimental.pallas import tpu as pltpu
from jax.sharding import PartitionSpec as P

EPSILON = 1e-05
MESH = pl.DeviceIdType.MESH
F32 = jnp.float32
BF16 = jnp.bfloat16

XN, ZN, YN = 4, 8, 4
GN = XN * ZN
ND = 128
D = 512
EDGES = 1024
SLOTS = 32
BM = 256
NB = EDGES // BM
VMEM_LIMIT = 56 * 1024 * 1024

RING_ORDER = (0, 1, 5, 2, 6, 3, 7, 4)
RING_OFFSET = (0, -1, -2, -3, -4, 1, 2, 3)


def nn(left, right):
    return jnp.dot(left, right, preferred_element_type=F32)


def nt(left, right):
    return lax.dot_general(left, right, (((1,), (1,)), ((), ())), preferred_element_type=F32)


def tn(left, right):
    return lax.dot_general(left, right, (((0,), (0,)), ((), ())), preferred_element_type=F32)


def place():
    dp = lax.axis_index("dp")
    graph = lax.axis_index("graph")
    return dp, graph // ZN, graph % ZN


def remote(src, dst, send, recv, device):
    return pltpu.make_async_remote_copy(
        src_ref=src, dst_ref=dst, send_sem=send, recv_sem=recv, device_id=device, device_id_type=MESH
    )


def enter(devices):
    barrier = pltpu.get_barrier_semaphore()
    for device in devices:
        pl.semaphore_signal(barrier, inc=1, device_id=device, device_id_type=MESH)
    pl.semaphore_wait(barrier, len(devices))


def onehot_rows(count, row):
    index = lax.broadcasted_iota(jnp.int32, (count, row.shape[1]), 0)
    return jnp.where(index == row, 1.0, 0.0).astype(BF16)


def normalize(values):
    average = jnp.mean(values, -1, keepdims=True)
    centered = values - average
    inverse = lax.rsqrt(jnp.mean(centered * centered, -1, keepdims=True) + EPSILON)
    return centered * inverse, inverse


def norm_backward(upstream, normed, inverse, scales):
    scaled = upstream * scales
    return inverse * (
        scaled
        - jnp.mean(scaled, -1, keepdims=True)
        - normed * jnp.mean(scaled * normed, -1, keepdims=True)
    )


def sigmoid(values):
    return 0.5 + 0.5 * jnp.tanh(0.5 * values)


REDUCE_ORDER = (4, 7, 3, 6, 2, 5, 1, 0)
REDUCE_OFFSET = (0, 1, 2, 3, 4, -1, -2, -3)
PARTS = 2
CHUNK = 256


def hot_columns(column, count):
    index = lax.broadcasted_iota(jnp.int32, (column.shape[0], count), 1)
    return jnp.where(index == column, 1.0, 0.0).astype(BF16)


def columns_of(rows):
    padded = jnp.concatenate([rows.astype(F32), jnp.zeros((128 - rows.shape[0], 128), F32)], axis=0)
    return padded.T.astype(jnp.int32)


def layer_kernel(
    counts_ref,
    node_ref,
    senders_ref,
    recv_ref,
    vectors_ref,
    edge_hbm,
    edge_first_hbm,
    edge_second_hbm,
    node_first_hbm,
    node_second_hbm,
    node_cot_hbm,
    edge_cot_hbm,
    new_nodes_hbm,
    new_edges_hbm,
    edge_grad_hbm,
    node_grad_ref,
    final_edge,
    final_node,
    sums_ref,
    held,
):
    s = SimpleNamespace(**held)
    dp, x, z = place()
    graph = x * ZN + z
    y, core = dp // 2, dp % 2
    partner = (y * 2 + (1 - core), graph)
    x_peers = [None] + [(dp, ((x + k) % XN) * ZN + z) for k in range(1, XN)]
    z_peers = [None] + [(dp, x * ZN + (z + k) % ZN) for k in range(1, ZN)]
    y_peers = [None] + [(((y + k) % YN) * 2 + core, graph) for k in range(1, YN)]
    dp_peers = [None] + [((dp + k) % 8, graph) for k in range(1, 8)]
    up, down = z_peers[1], z_peers[ZN - 1]

    loads = {}
    for index, (hbm, ref) in enumerate(
        (
            (edge_first_hbm, s.edge_first),
            (edge_hbm, s.edges),
            (edge_second_hbm, s.edge_second),
            (node_first_hbm, s.node_first),
            (node_second_hbm, s.node_second),
            (node_cot_hbm, s.node_cot),
            (edge_cot_hbm, s.edge_cot),
        )
    ):
        loads[index] = pltpu.make_async_copy(hbm, ref, s.load_sem.at[index])
        loads[index].start()
    edges, edge_first, edge_second = s.edges, s.edge_first, s.edge_second
    node_first, node_second = s.node_first, s.node_second
    edge_cot, node_cot = s.edge_cot, s.node_cot

    enter(x_peers[1:] + z_peers[1:] + dp_peers[1:])
    sent = []

    def start(src, dst, sems, index, device):
        copy = remote(src, dst, sems[0].at[index], sems[1].at[index], device)
        copy.start()
        sent.append(copy)
        return copy

    ring, buf = s.ring, s.buf
    rows_of = ND // PARTS

    def hop(src, slot, device, part):
        piece = pl.ds(part * rows_of, rows_of)
        return start(src.at[piece], ring.at[slot, piece], s.hop_sems, (slot, part), device)

    hops = {}
    for part in range(PARTS):
        hops[1, part] = hop(node_ref, 1, up, part)
        hops[5, part] = hop(node_ref, 5, down, part)

    senders = senders_ref[...]
    owners = senders // ND
    local = (senders % ND).astype(F32)
    earlier = jnp.where(
        lax.broadcasted_iota(jnp.int32, (ND, ND), 0) < lax.broadcasted_iota(jnp.int32, (ND, ND), 1), 1.0, 0.0
    ).astype(BF16)
    base = jnp.zeros((GN, 1), F32)
    table = jnp.zeros((GN, ND), F32)
    lane = lax.broadcasted_iota(jnp.int32, (ND, ND), 0)
    group = lax.broadcasted_iota(jnp.int32, (GN, ND), 0)
    slot_rows = []
    for b in range(EDGES // ND):
        owner = owners[b : b + 1, :]
        mine = jnp.where(group == owner, 1.0, 0.0)
        before = nn(mine.astype(BF16), earlier) + base
        rank = jnp.sum(mine * before, axis=0, keepdims=True).astype(jnp.int32)
        base = base + jnp.sum(mine, axis=1, keepdims=True)
        slot_rows.append(owner * SLOTS + rank)
        column = jnp.where(lane == rank + SLOTS * x, 1.0, 0.0).astype(BF16)
        table = table + nt((mine * local[b : b + 1, :]).astype(BF16), column)
    lists_own, lists_in, lists = s.lists_own, s.lists_in, s.lists
    lists_own[...] = table.reshape(XN, ZN, ND)
    list_copies = [
        start(lists_own.at[(x + k) % XN], lists_in.at[k - 1], s.list_sems, k - 1, x_peers[k]) for k in range(1, XN)
    ]
    slot_columns = columns_of(jnp.concatenate(slot_rows, axis=0))
    recv = recv_ref[...] - graph * ND
    recv_columns = columns_of(recv)
    perm, perm_back, hot, hot_back, slope = s.perm, s.perm_back, s.hot, s.hot_back, s.slope
    h = node_ref[...]

    def fill(step):
        if step == 0:
            loads[0].wait()
            s.h_recv[...] = nn(h, edge_first[2]).astype(BF16)
        elif step == 1:
            loads[1].wait()
        if 1 <= step <= NB:
            i = step - 1
            rows = slice(i * BM, (i + 1) * BM)
            for b in range(i * BM // 128, (i + 1) * BM // 128):
                block = slice(b * 128, (b + 1) * 128)
                perm[block, :] = hot_columns(slot_columns[:, b : b + 1], EDGES)
                perm_back[:, block] = onehot_rows(EDGES, slot_rows[b])
                hot[block, :] = hot_columns(recv_columns[:, b : b + 1], ND)
                hot_back[:, block] = onehot_rows(ND, recv[b : b + 1, :])
            slope[rows, :] = (
                nn(edges[rows, :], edge_first[0]) + nn(hot[rows, :], s.h_recv[...]) + vectors_ref[0:1, :]
            )

    stage = s.stage
    x_copies = []

    def forward(slot, part):
        hops[slot, part].wait_recv()
        if slot in (1, 2, 3):
            hops[slot + 1, part] = hop(ring.at[slot], slot + 1, up, part)
        elif slot in (5, 6):
            hops[slot + 1, part] = hop(ring.at[slot], slot + 1, down, part)

    def relay(slot):
        source = (z + RING_OFFSET[slot] + ZN) % ZN
        chosen = onehot_rows(ND, lists[pl.ds(source, 1), :])
        stage[slot] = tn(chosen, ring[slot] if slot else h).astype(BF16).reshape(XN, SLOTS, D)
        for k in range(1, XN):
            x_copies.append(
                start(stage.at[slot, (x + k) % XN], buf.at[x * ZN + source], s.away_sems, (slot, k - 1), x_peers[k])
            )
        buf[x * ZN + source] = stage[slot, x]

    fill(0)
    for copy in list_copies:
        copy.wait_recv()
    lists[...] = (lists_own[x] + lists_in[0] + lists_in[1] + lists_in[2]).astype(jnp.int32)
    for step, slots in enumerate(((1, 5), (2, 6), (3, 7), (4,)), 1):
        for part in range(PARTS):
            for slot in slots:
                forward(slot, part)
        for slot in slots if step > 1 else (0,) + slots:
            relay(slot)
        fill(step)
    for index in range(2, 7):
        loads[index].wait()
    for copy in x_copies:
        copy.wait_recv()

    live_rows = counts_ref[0] * 128
    act, normed, inverse, new_edges = s.act, s.normed, s.inverse, s.new_edges
    aggregate = jnp.zeros((ND, D), F32)
    for i in range(NB):
        rows = slice(i * BM, (i + 1) * BM)
        sent_rows = nn(perm[rows, :], buf[...].reshape(EDGES, D)).astype(BF16)
        pre = slope[rows, :] + nn(sent_rows, edge_first[1])
        gate = sigmoid(pre)
        act_b = (pre * gate).astype(BF16)
        act[rows, :] = act_b
        slope[rows, :] = gate * (1.0 + pre * (1.0 - gate))
        hat, inv = normalize(nn(act_b, edge_second[...]))
        normed[rows, :] = hat
        inverse[rows, :] = inv
        live = lax.broadcasted_iota(jnp.int32, (BM, 1), 0) + i * BM < live_rows
        message = jnp.where(live, hat * vectors_ref[2:3, :], 0.0).astype(BF16)
        new_edges[rows, :] = (edges[rows, :].astype(F32) + message.astype(F32)).astype(BF16)
        aggregate = aggregate + nn(hot_back[:, rows], message)
    store_edges = pltpu.make_async_copy(new_edges, new_edges_hbm, s.store_sem.at[0])
    store_edges.start()
    aggregate = aggregate.astype(BF16)

    grads = s.grads
    node_pre = nn(h, node_first[0]) + nn(aggregate, node_first[1]) + vectors_ref[1:2, :]
    node_gate = sigmoid(node_pre)
    node_act = (node_pre * node_gate).astype(BF16)
    node_hat, node_inv = normalize(nn(node_act, node_second[...]))
    s.new_nodes[...] = (h.astype(F32) + node_hat * vectors_ref[3:4, :]).astype(BF16)
    store_nodes = pltpu.make_async_copy(s.new_nodes, new_nodes_hbm, s.store_sem.at[1])
    store_nodes.start()
    upstream = node_cot[...].astype(F32)
    node_dz = norm_backward(upstream, node_hat, node_inv, vectors_ref[3:4, :]).astype(BF16)
    node_dpre = (
        nt(node_dz, node_second[...]) * (node_gate * (1.0 + node_pre * (1.0 - node_gate)))
    ).astype(BF16)
    aggregate_cot = nt(node_dpre, node_first[1]).astype(BF16)
    col_node = jnp.sum(node_dpre.astype(F32), 0, keepdims=True)
    col_node_scale = jnp.sum(upstream * node_hat, 0, keepdims=True)
    grads[4] = tn(h, node_dpre).astype(BF16)
    grads[5] = tn(aggregate, node_dpre).astype(BF16)
    grads[6] = tn(node_act, node_dz).astype(BF16)
    s.node_part[...] = upstream + nt(node_dpre, node_first[0])

    def make(src, dst, sems, index, device):
        return remote(src, dst, sems[0].at[index], sems[1].at[index], device)

    def row_chunk(index):
        return pl.ds(pl.multiple_of(index * 128, 128), 128)

    class Share:
        def __init__(self, owner, first, count, held, final):
            t = SimpleNamespace(**held)
            self.owner, self.first, self.count, self.final = owner, first, count, final
            self.core_in, self.pair = t.core_in, t.pair
            self.a_in, self.a_sum = t.a_in, t.a_sum
            self.b_in, self.b_sum, self.z_in = t.b_in, t.b_sum, t.z_in
            columns_first = owner == 0
            if columns_first:
                self.a_place, self.b_place, a_peers, b_peers = y, x, y_peers, x_peers
                self.cuts = [(slice(None), slice(j * 128, (j + 1) * 128)) for j in range(4)]
            else:
                self.a_place, self.b_place, a_peers, b_peers = x, y, x_peers, y_peers
                self.cuts = [(slice(j * 128, (j + 1) * 128), slice(None)) for j in range(4)]

            def b_cut(k):
                piece = row_chunk((self.b_place + k) % 4)
                return (slice(None), piece, slice(None)) if columns_first else (slice(None), slice(None), piece)

            self.b_own = b_cut(0)
            self.core_copies = [
                make(grads.at[first + m], self.core_in.at[m], t.core_sems, m, partner) for m in range(count)
            ]
            self.a_copies = [
                [
                    make(self.pair.at[(self.a_place + k) % 4, m], self.a_in.at[k - 1, m], t.a_sems, (k - 1, m), a_peers[k])
                    for k in (2, 1, 3)
                ]
                for m in range(count)
            ]
            self.b_copies = [
                make(self.a_sum.at[b_cut(k)], self.b_in.at[k - 1], t.b_sems, k - 1, b_peers[k]) for k in (2, 1, 3)
            ]
            self.z_copies = [
                make(
                    self.b_sum.at[:, pl.ds(pl.multiple_of(((z + k) % ZN) * 16, 16), 16), :],
                    self.z_in.at[k - 1],
                    t.z_sems,
                    k - 1,
                    z_peers[k],
                )
                for k in (4, 3, 5, 2, 6, 1, 7)
            ]
            self.dp_copies = [
                remote(final.at[y], final.at[y], t.dp_sems[0].at[k - 1], t.dp_sems[1].at[y], dp_peers[k])
                for k in range(1, 8)
            ]
            self.dp_in = [
                remote(
                    final.at[(y + k) % YN],
                    final.at[(y + k) % YN],
                    t.dp_sems[0].at[0],
                    t.dp_sems[1].at[(y + k) % YN],
                    dp_peers[1],
                )
                for k in range(YN)
            ]

        def give(self, m):
            @pl.when(core != self.owner)
            def _():
                self.core_copies[m].start()

        def across_a(self, m):
            @pl.when(core == self.owner)
            def _():
                self.core_copies[m].wait_recv()
                for j, (rows, lanes) in enumerate(self.cuts):
                    self.pair[j, m] = (
                        grads[self.first + m, rows, lanes].astype(F32) + self.core_in[m, rows, lanes].astype(F32)
                    ).astype(BF16)
                for copy in self.a_copies[m]:
                    copy.start()

        def across_b(self):
            @pl.when(core == self.owner)
            def _():
                for m in range(self.count):
                    for copy in self.a_copies[m]:
                        copy.wait_recv()
                    self.a_sum[m] = (
                        self.pair[self.a_place, m].astype(F32)
                        + self.a_in[0, m].astype(F32)
                        + self.a_in[1, m].astype(F32)
                        + self.a_in[2, m].astype(F32)
                    ).astype(BF16)
                for copy in self.b_copies:
                    copy.start()

        def across_z(self):
            @pl.when(core == self.owner)
            def _():
                for copy in self.b_copies:
                    copy.wait_recv()
                self.b_sum[...] = (
                    self.a_sum[self.b_own].astype(F32)
                    + self.b_in[0].astype(F32)
                    + self.b_in[1].astype(F32)
                    + self.b_in[2].astype(F32)
                ).astype(BF16)
                for copy in self.z_copies:
                    copy.start()

        def across_dp(self):
            @pl.when(core == self.owner)
            def _():
                for copy in self.z_copies:
                    copy.wait_recv()
                total = self.b_sum[:, pl.ds(pl.multiple_of(z * 16, 16), 16), :].astype(F32)
                for k in range(ZN - 1):
                    total = total + self.z_in[k].astype(F32)
                self.final[y] = total.astype(BF16)
                for copy in self.dp_copies:
                    copy.start()

        def finish(self):
            for k in range(YN):
                if k:
                    self.dp_in[k].wait_recv()
                else:

                    @pl.when(core != self.owner)
                    def _():
                        self.dp_in[0].wait_recv()

        def drain(self):
            @pl.when(core != self.owner)
            def _():
                for copy in self.core_copies:
                    copy.wait_send()

            @pl.when(core == self.owner)
            def _():
                for copies in self.a_copies:
                    for copy in copies:
                        copy.wait_send()
                for copy in self.b_copies + self.z_copies + self.dp_copies:
                    copy.wait_send()

    node_share = Share(1, 4, 3, s.node_share, final_node)
    edge_share = Share(0, 0, 4, s.edge_share, final_edge)
    for m in range(3):
        node_share.give(m)

    dz, dpre = s.dz, s.dpre
    col_scale = jnp.zeros((1, D), F32)
    for i in range(NB):
        rows = slice(i * BM, (i + 1) * BM)
        live = lax.broadcasted_iota(jnp.int32, (BM, 1), 0) + i * BM < live_rows
        message_cot = jnp.where(live, edge_cot[rows, :].astype(F32) + nn(hot[rows, :], aggregate_cot), 0.0)
        hat = normed[rows, :]
        col_scale = col_scale + jnp.sum(message_cot * hat, 0, keepdims=True)
        dz[rows, :] = norm_backward(message_cot, hat, inverse[rows, :], vectors_ref[2:3, :]).astype(BF16)
        if i == NB // 2 - 1:
            for m in range(3):
                node_share.across_a(m)
    grads[3] = tn(act[...], dz[...]).astype(BF16)
    edge_share.give(3)
    col_edge = jnp.zeros((1, D), F32)
    received = jnp.zeros((ND, D), F32)
    for i in range(NB):
        rows = slice(i * BM, (i + 1) * BM)
        dpre_b = (nt(dz[rows, :], edge_second[...]) * slope[rows, :]).astype(BF16)
        dpre[rows, :] = dpre_b
        col_edge = col_edge + jnp.sum(dpre_b.astype(F32), 0, keepdims=True)
        received = received + nn(hot_back[:, rows], dpre_b)
    received = received.astype(BF16)
    edge_share.across_a(3)
    grads[2] = tn(h, received).astype(BF16)
    edge_share.give(2)
    grads[0] = tn(edges[...], dpre[...]).astype(BF16)
    edge_share.give(0)
    back = s.back
    back[...] = nn(perm_back[...], dpre[...]).astype(BF16).reshape(GN, SLOTS, D)
    rows_in = s.rows_in
    row_copies = {}
    for j in REDUCE_ORDER:
        target = (z + REDUCE_OFFSET[j] + ZN) % ZN
        row_copies[j] = [
            start(back.at[((x + k) % XN) * ZN + target], rows_in.at[j, x], s.row_sems, (j, k - 1), x_peers[k])
            for k in range(1, XN)
        ]
    edge_share.across_a(2)
    grads[1] = tn(buf[...].reshape(EDGES, D), back[...].reshape(EDGES, D)).astype(BF16)
    edge_share.give(1)
    edge_share.across_a(0)

    sums = s.sums
    sums[0] = jnp.concatenate([col_edge, col_node, col_scale, col_node_scale, jnp.zeros((4, D), F32)], axis=0)
    dp_sums = [start(sums.at[0], s.dp_sums.at[k - 1], s.sdp_sems, k - 1, dp_peers[k]) for k in range(1, 8)]
    for j in REDUCE_ORDER:
        target = (z + REDUCE_OFFSET[j] + ZN) % ZN
        rows_in[j, x] = back[x * ZN + target]
    edge_share.across_a(1)
    node_share.across_b()

    ring_out, ring_in = s.ring_out, s.ring_in
    ring_copies = {}

    def ring_step(j):
        target = (z + REDUCE_OFFSET[j] + ZN) % ZN
        for copy in row_copies[j]:
            copy.wait_recv()
        total = nn(onehot_rows(ND, lists[pl.ds(target, 1), :]), rows_in[j].reshape(ND, D))
        if j:
            for part in range(PARTS):
                piece = slice(part * rows_of, (part + 1) * rows_of)
                partial = total[piece]
                if j in (3, 2, 1, 6, 5):
                    ring_copies[j + 1, part].wait_recv()
                    partial = partial + ring_in[j + 1, piece].astype(F32)
                ring_out[j, piece] = partial.astype(BF16)
                ring_copies[j, part] = start(
                    ring_out.at[j, piece], ring_in.at[j, piece], s.back_sems, (j, part), up if j < 5 else down
                )
            return
        for part in range(PARTS):
            ring_copies[1, part].wait_recv()
            ring_copies[5, part].wait_recv()
        total = total + ring_in[1].astype(F32) + ring_in[5].astype(F32)
        node_grad_ref[...] = (
            s.node_part[...] + nt(total.astype(BF16), edge_first[1]) + nt(received, edge_first[2])
        ).astype(BF16)

    def sum_step(parts, source, index):
        total = sums[source]
        for k in range(parts.shape[0]):
            total = total + parts[k]
        sums[index] = total

    edge_grad = s.edge_grad
    for i in range(NB):
        rows = slice(i * BM, (i + 1) * BM)
        edge_grad[rows, :] = (edge_cot[rows, :].astype(F32) + nt(dpre[rows, :], edge_first[0])).astype(BF16)
        if i % 2:
            ring_step(REDUCE_ORDER[i // 2])
    store_grad = pltpu.make_async_copy(edge_grad, edge_grad_hbm, s.store_sem.at[2])
    store_grad.start()
    for copy in dp_sums:
        copy.wait_recv()
    sum_step(s.dp_sums, 0, 1)
    x_sums = [start(sums.at[1], s.x_sums.at[k - 1], s.sx_sems, k - 1, x_peers[k]) for k in range(1, XN)]
    ring_step(3)
    ring_step(6)
    node_share.across_z()
    ring_step(2)
    ring_step(5)
    edge_share.across_b()
    for copy in x_sums:
        copy.wait_recv()
    sum_step(s.x_sums, 1, 2)
    z_sums = [start(sums.at[2], s.z_sums.at[k - 1], s.sz_sems, k - 1, z_peers[k]) for k in range(1, ZN)]
    ring_step(1)
    node_share.across_dp()
    edge_share.across_z()
    ring_step(0)
    for copy in z_sums:
        copy.wait_recv()
    sum_step(s.z_sums, 2, 3)
    sums_ref[...] = sums[3]
    node_share.finish()
    edge_share.across_dp()
    store_edges.wait()
    store_nodes.wait()
    store_grad.wait()
    for copy in sent:
        copy.wait_send()
    edge_share.finish()
    node_share.drain()
    edge_share.drain()


def scratch():
    v, dma = pltpu.VMEM, pltpu.SemaphoreType.DMA

    def pair(*size):
        return dma(size), dma(size)

    def share(count, a_shape):
        return dict(
            core_in=v((count, D, D), BF16),
            pair=v((4, count) + a_shape, BF16),
            a_in=v((3, count) + a_shape, BF16),
            a_sum=v((count,) + a_shape, BF16),
            b_in=v((3, count, 128, 128), BF16),
            b_sum=v((count, 128, 128), BF16),
            z_in=v((ZN - 1, count, 16, 128), BF16),
            core_sems=pair(count),
            a_sems=pair(3, count),
            b_sems=pair(3),
            z_sems=pair(ZN - 1),
            dp_sems=(dma((7,)), dma((YN,))),
        )

    return dict(
        edges=v((EDGES, D), BF16),
        edge_first=v((3, D, D), BF16),
        edge_second=v((D, D), BF16),
        node_first=v((2, D, D), BF16),
        node_second=v((D, D), BF16),
        node_cot=v((ND, D), BF16),
        edge_cot=v((EDGES, D), BF16),
        load_sem=dma((7,)),
        store_sem=dma((3,)),
        ring=v((ZN, ND, D), BF16),
        stage=v((ZN, XN, SLOTS, D), BF16),
        buf=v((GN, SLOTS, D), BF16),
        lists_own=v((XN, ZN, ND), F32),
        lists_in=v((XN - 1, ZN, ND), F32),
        lists=v((ZN, ND), jnp.int32),
        perm=v((EDGES, EDGES), BF16),
        perm_back=v((EDGES, EDGES), BF16),
        hot=v((EDGES, ND), BF16),
        hot_back=v((ND, EDGES), BF16),
        h_recv=v((ND, D), BF16),
        act=v((EDGES, D), BF16),
        slope=v((EDGES, D), F32),
        normed=v((EDGES, D), F32),
        inverse=v((EDGES, 1), F32),
        new_edges=v((EDGES, D), BF16),
        new_nodes=v((ND, D), BF16),
        edge_grad=v((EDGES, D), BF16),
        node_part=v((ND, D), F32),
        dz=v((EDGES, D), BF16),
        dpre=v((EDGES, D), BF16),
        back=v((GN, SLOTS, D), BF16),
        rows_in=v((ZN, XN, SLOTS, D), BF16),
        ring_out=v((ZN, ND, D), BF16),
        ring_in=v((ZN, ND, D), BF16),
        grads=v((7, D, D), BF16),
        sums=v((4, 8, D), F32),
        dp_sums=v((7, 8, D), F32),
        x_sums=v((XN - 1, 8, D), F32),
        z_sums=v((ZN - 1, 8, D), F32),
        hop_sems=pair(ZN, PARTS),
        list_sems=pair(XN - 1),
        away_sems=pair(ZN, XN - 1),
        row_sems=pair(ZN, XN - 1),
        back_sems=pair(ZN, PARTS),
        sdp_sems=pair(7),
        sx_sems=pair(XN - 1),
        sz_sems=pair(ZN - 1),
        edge_share=share(4, (D, 128)),
        node_share=share(3, (128, D)),
    )


def layer(counts, node, senders, recv, vectors, edges, edge_first, edge_second, node_first, node_second, node_cot, edge_cot):
    vmem = pl.BlockSpec(memory_space=pltpu.VMEM)
    hbm = pl.BlockSpec(memory_space=pl.ANY)
    return pl.pallas_call(
        layer_kernel,
        out_shape=(
            jax.ShapeDtypeStruct((ND, D), BF16),
            jax.ShapeDtypeStruct((EDGES, D), BF16),
            jax.ShapeDtypeStruct((EDGES, D), BF16),
            jax.ShapeDtypeStruct((ND, D), BF16),
            jax.ShapeDtypeStruct((YN, 4, 16, 128), BF16),
            jax.ShapeDtypeStruct((YN, 3, 16, 128), BF16),
            jax.ShapeDtypeStruct((8, D), F32),
        ),
        in_specs=[pl.BlockSpec(memory_space=pltpu.SMEM)] + [vmem] * 4 + [hbm] * 7,
        out_specs=(hbm,) * 3 + (vmem,) * 4,
        scratch_shapes=[scratch()],
        compiler_params=pltpu.CompilerParams(
            collective_id=0, has_side_effects=True, vmem_limit_bytes=VMEM_LIMIT
        ),
        name="layer",
    )(counts, node, senders, recv, vectors, edges, edge_first, edge_second, node_first, node_second, node_cot, edge_cot)


def outputs_kernel(
    nodes_in,
    edges_in,
    edge_grad_in,
    node_grad_in,
    edge_part,
    node_part,
    sums_ref,
    nodes_out,
    edges_out,
    edge_grad_out,
    node_grad_out,
    edge_first_ref,
    edge_second_ref,
    node_first_ref,
    node_second_ref,
    vectors_ref,
    edges_held,
    edge_grad_held,
    nodes_held,
    node_grad_held,
    in_sems,
    out_sems,
):
    moves = []
    for src, held, dst in (
        (edges_in, edges_held, edges_out),
        (edge_grad_in, edge_grad_held, edge_grad_out),
        (nodes_in, nodes_held, nodes_out),
        (node_grad_in, node_grad_held, node_grad_out),
    ):
        size = min(CHUNK, src.shape[0])
        for first in range(0, src.shape[0], size):
            piece, index = pl.ds(first, size), len(moves)
            moves.append(
                (
                    pltpu.make_async_copy(src.at[piece], held.at[piece], in_sems.at[index]),
                    pltpu.make_async_copy(held.at[piece], dst.at[piece], out_sems.at[index]),
                )
            )
    for fetch, _ in moves:
        fetch.start()
    for j in range(YN):
        lanes = slice(j * 128, (j + 1) * 128)
        for m in range(3):
            edge_first_ref[m, :, lanes] = edge_part[j, m].astype(F32)
        edge_second_ref[:, lanes] = edge_part[j, 3].astype(F32)
        for m in range(2):
            node_first_ref[m, :, lanes] = node_part[j, m].astype(F32)
        node_second_ref[:, lanes] = node_part[j, 2].astype(F32)
    shift = (D - lax.axis_index("graph") * 16) % D
    vectors_ref[...] = pltpu.roll(sums_ref[...], shift, 1)[0:4, 0:16]
    for fetch, store in moves:
        fetch.wait()
        store.start()
    for _, store in moves:
        store.wait()


def outputs(nodes, edges, edge_grad, node_grad, edge_part, node_part, sums):
    vmem = pl.BlockSpec(memory_space=pltpu.VMEM)
    hbm = pl.BlockSpec(memory_space=pl.ANY)
    return pl.pallas_call(
        outputs_kernel,
        out_shape=(
            jax.ShapeDtypeStruct((ND, D), BF16),
            jax.ShapeDtypeStruct((EDGES, D), BF16),
            jax.ShapeDtypeStruct((EDGES, D), BF16),
            jax.ShapeDtypeStruct((ND, D), BF16),
            jax.ShapeDtypeStruct((3, 16, D), F32),
            jax.ShapeDtypeStruct((16, D), F32),
            jax.ShapeDtypeStruct((2, 16, D), F32),
            jax.ShapeDtypeStruct((16, D), F32),
            jax.ShapeDtypeStruct((4, 16), F32),
        ),
        in_specs=[hbm] * 4 + [vmem] * 3,
        out_specs=(hbm,) * 4 + (vmem,) * 5,
        scratch_shapes=[
            pltpu.VMEM((EDGES, D), BF16),
            pltpu.VMEM((EDGES, D), BF16),
            pltpu.VMEM((ND, D), BF16),
            pltpu.VMEM((ND, D), BF16),
            pltpu.SemaphoreType.DMA((2 * EDGES // CHUNK + 2,)),
            pltpu.SemaphoreType.DMA((2 * EDGES // CHUNK + 2,)),
        ],
        compiler_params=pltpu.CompilerParams(vmem_limit_bytes=VMEM_LIMIT),
        name="outputs",
    )(nodes, edges, edge_grad, node_grad, edge_part, node_part, sums)


def body(
    node_latents,
    edge_latents,
    senders,
    receivers,
    block_counts,
    edge_first,
    edge_second,
    node_first,
    node_second,
    vectors,
    node_cotangent,
    edge_cotangent,
):
    new_nodes, new_edges, edge_grad, node_grad, edge_part, node_part, sums = layer(
        block_counts,
        node_latents[0],
        senders,
        receivers,
        vectors,
        edge_latents.reshape(EDGES, D),
        edge_first,
        edge_second,
        node_first,
        node_second,
        node_cotangent[0],
        edge_cotangent.reshape(EDGES, D),
    )
    new_nodes, new_edges, edge_grad, node_grad, grad_ef, grad_es, grad_nf, grad_ns, columns = outputs(
        new_nodes, new_edges, edge_grad, node_grad, edge_part, node_part, sums
    )
    shape = edge_latents.shape
    return (
        new_nodes[None],
        new_edges.reshape(shape),
        node_grad[None],
        edge_grad.reshape(shape),
        grad_ef,
        grad_es,
        grad_nf,
        grad_ns,
        columns,
    )


def solution(mesh):
    return jax.shard_map(
        body,
        mesh=mesh,
        in_specs=(
            P("dp", "graph", None),
            P("dp", "graph", None, None),
            P("graph", None),
            P("graph", None),
            P("graph"),
            P(),
            P(),
            P(),
            P(),
            P(),
            P("dp", "graph", None),
            P("dp", "graph", None, None),
        ),
        out_specs=(
            P("dp", "graph", None),
            P("dp", "graph", None, None),
            P("dp", "graph", None),
            P("dp", "graph", None, None),
            P(None, "graph", None),
            P("graph", None),
            P(None, "graph", None),
            P("graph", None),
            P(None, "graph"),
        ),
        check_vma=False,
    )
```

```python
from types import SimpleNamespace

import jax
import jax.numpy as jnp
from jax import lax
from jax.experimental import pallas as pl
from jax.experimental.pallas import tpu as pltpu
from jax.sharding import PartitionSpec as P

EPSILON = 1e-05
MESH = pl.DeviceIdType.MESH
F32 = jnp.float32
BF16 = jnp.bfloat16

XN, ZN, YN = 4, 8, 4
GN = XN * ZN
ND = 128
D = 512
EDGES = 1024
SLOTS = 32
BM = 512
NB = EDGES // BM
VMEM_LIMIT = 56 * 1024 * 1024

RING_ORDER = (0, 1, 5, 2, 6, 3, 7, 4)
RING_OFFSET = (0, -1, -2, -3, -4, 1, 2, 3)


def nn(left, right):
    return jnp.dot(left, right, preferred_element_type=F32)


def nt(left, right):
    return lax.dot_general(left, right, (((1,), (1,)), ((), ())), preferred_element_type=F32)


def tn(left, right):
    return lax.dot_general(left, right, (((0,), (0,)), ((), ())), preferred_element_type=F32)


def place():
    dp = lax.axis_index("dp")
    graph = lax.axis_index("graph")
    return dp, graph // ZN, graph % ZN


def remote(src, dst, send, recv, device):
    return pltpu.make_async_remote_copy(
        src_ref=src, dst_ref=dst, send_sem=send, recv_sem=recv, device_id=device, device_id_type=MESH
    )


def onehot_rows(count, row):
    index = lax.broadcasted_iota(jnp.int32, (count, row.shape[1]), 0)
    return jnp.where(index == row, 1.0, 0.0).astype(BF16)


def normalize(values):
    average = jnp.mean(values, -1, keepdims=True)
    centered = values - average
    inverse = lax.rsqrt(jnp.mean(centered * centered, -1, keepdims=True) + EPSILON)
    return centered * inverse, inverse


def norm_backward(upstream, normed, inverse, scales):
    scaled = upstream * scales
    return inverse * (
        scaled
        - jnp.mean(scaled, -1, keepdims=True)
        - normed * jnp.mean(scaled * normed, -1, keepdims=True)
    )


def sigmoid(values):
    return 0.5 + 0.5 * jnp.tanh(0.5 * values)


REDUCE_ORDER = (4, 7, 3, 6, 2, 5, 1, 0)
REDUCE_OFFSET = (0, 1, 2, 3, 4, -1, -2, -3)
PARTS = 2
CHUNK = 256


def hot_columns(column, count):
    index = lax.broadcasted_iota(jnp.int32, (column.shape[0], count), 1)
    return jnp.where(index == column, 1.0, 0.0).astype(BF16)


def columns_of(rows):
    padded = jnp.concatenate([rows.astype(F32), jnp.zeros((128 - rows.shape[0], 128), F32)], axis=0)
    return padded.T.astype(jnp.int32)


def layer_kernel(
    counts_ref,
    node_hbm,
    senders_hbm,
    recv_hbm,
    vectors_hbm,
    edge_hbm,
    edge_first_hbm,
    edge_second_hbm,
    node_first_hbm,
    node_second_hbm,
    node_cot_hbm,
    edge_cot_hbm,
    new_nodes_hbm,
    new_edges_hbm,
    edge_grad_hbm,
    node_grad_ref,
    final_edge,
    final_node,
    sums_ref,
    held,
):
    s = SimpleNamespace(**held)
    dp, x, z = place()
    graph = x * ZN + z
    y, core = dp // 2, dp % 2
    partner = (y * 2 + (1 - core), graph)
    x_peers = [None] + [(dp, ((x + k) % XN) * ZN + z) for k in range(1, XN)]
    z_peers = [None] + [(dp, x * ZN + (z + k) % ZN) for k in range(1, ZN)]
    y_peers = [None] + [(((y + k) % YN) * 2 + core, graph) for k in range(1, YN)]
    dp_peers = [None] + [((dp + k) % 8, graph) for k in range(1, 8)]
    up, down = z_peers[1], z_peers[ZN - 1]

    peers = x_peers[1:] + z_peers[1:] + dp_peers[1:]
    barrier = pltpu.get_barrier_semaphore()
    for device in peers:
        pl.semaphore_signal(barrier, inc=1, device_id=device, device_id_type=MESH)

    node_ref, senders_ref, recv_ref, vectors_ref = s.node, s.senders, s.recv, s.vectors
    loads = {}
    for index, (hbm, ref) in enumerate(
        (
            (edge_first_hbm, s.edge_first),
            (edge_hbm, s.edges),
            (edge_second_hbm, s.edge_second),
            (node_first_hbm, s.node_first),
            (node_second_hbm, s.node_second),
            (node_cot_hbm, s.node_cot),
            (edge_cot_hbm, s.edge_cot),
            (node_hbm, s.node),
            (senders_hbm, s.senders),
            (recv_hbm, s.recv),
            (vectors_hbm, s.vectors),
        )
    ):
        loads[index] = pltpu.make_async_copy(hbm, ref, s.load_sem.at[index])
    for index in (7, 8, 9, 10, 0, 1, 2, 3, 4, 5, 6):
        loads[index].start()
    edges, edge_first, edge_second = s.edges, s.edge_first, s.edge_second
    node_first, node_second = s.node_first, s.node_second
    edge_cot, node_cot = s.edge_cot, s.node_cot

    loads[7].wait()
    pl.semaphore_wait(barrier, len(peers))
    sent = []

    def start(src, dst, sems, index, device):
        copy = remote(src, dst, sems[0].at[index], sems[1].at[index], device)
        copy.start()
        sent.append(copy)
        return copy

    ring, buf = s.ring, s.buf
    rows_of = ND // PARTS

    def hop(src, slot, device, part):
        piece = pl.ds(part * rows_of, rows_of)
        return start(src.at[piece], ring.at[slot, piece], s.hop_sems, (slot, part), device)

    hops = {}
    for part in range(PARTS):
        hops[1, part] = hop(node_ref, 1, up, part)
        hops[5, part] = hop(node_ref, 5, down, part)

    for index in (8, 9, 10):
        loads[index].wait()
    senders = senders_ref[...]
    owners = senders // ND
    local = (senders % ND).astype(F32)
    earlier = jnp.where(
        lax.broadcasted_iota(jnp.int32, (ND, ND), 0) < lax.broadcasted_iota(jnp.int32, (ND, ND), 1), 1.0, 0.0
    ).astype(BF16)
    base = jnp.zeros((GN, 1), F32)
    table = jnp.zeros((GN, ND), F32)
    lane = lax.broadcasted_iota(jnp.int32, (ND, ND), 0)
    group = lax.broadcasted_iota(jnp.int32, (GN, ND), 0)
    slot_rows = []
    for b in range(EDGES // ND):
        owner = owners[b : b + 1, :]
        mine = jnp.where(group == owner, 1.0, 0.0)
        before = nn(mine.astype(BF16), earlier) + base
        rank = jnp.sum(mine * before, axis=0, keepdims=True).astype(jnp.int32)
        base = base + jnp.sum(mine, axis=1, keepdims=True)
        slot_rows.append(owner * SLOTS + rank)
        column = jnp.where(lane == rank + SLOTS * x, 1.0, 0.0).astype(BF16)
        table = table + nt((mine * local[b : b + 1, :]).astype(BF16), column)
    lists_own, lists_in, lists = s.lists_own, s.lists_in, s.lists
    lists_own[...] = table.reshape(XN, ZN, ND)
    list_copies = [
        start(lists_own.at[(x + k) % XN], lists_in.at[k - 1], s.list_sems, k - 1, x_peers[k]) for k in range(1, XN)
    ]
    slot_columns = columns_of(jnp.concatenate(slot_rows, axis=0))
    recv = recv_ref[...] - graph * ND
    recv_columns = columns_of(recv)
    perm, perm_back, hot, hot_back, slope = s.perm, s.perm_back, s.hot, s.hot_back, s.slope
    h = node_ref[...]

    def fill(step):
        if step == 0:
            loads[0].wait()
            s.h_recv[...] = nn(h, edge_first[2]).astype(BF16)
        elif step == 1:
            loads[1].wait()
        if 1 <= step <= NB:
            i = step - 1
            rows = slice(i * BM, (i + 1) * BM)
            for b in range(i * BM // 128, (i + 1) * BM // 128):
                block = slice(b * 128, (b + 1) * 128)
                perm[block, :] = hot_columns(slot_columns[:, b : b + 1], EDGES)
                perm_back[:, block] = onehot_rows(EDGES, slot_rows[b])
                hot[block, :] = hot_columns(recv_columns[:, b : b + 1], ND)
                hot_back[:, block] = onehot_rows(ND, recv[b : b + 1, :])
            slope[rows, :] = (
                nn(edges[rows, :], edge_first[0]) + nn(hot[rows, :], s.h_recv[...]) + vectors_ref[0:1, :]
            )

    stage = s.stage
    x_copies = []

    def forward(slot, part):
        hops[slot, part].wait_recv()
        if slot in (1, 2) or (slot == 3 and part == 0):
            hops[slot + 1, part] = hop(ring.at[slot], slot + 1, up, part)
        elif slot in (5, 6):
            hops[slot + 1, part] = hop(ring.at[slot], slot + 1, down, part)
        elif slot == 7 and part == 1:
            hops[4, part] = hop(ring.at[slot], 4, down, part)

    def relay(slot):
        source = (z + RING_OFFSET[slot] + ZN) % ZN
        chosen = onehot_rows(ND, lists[pl.ds(source, 1), :])
        stage[slot] = tn(chosen, ring[slot] if slot else h).astype(BF16).reshape(XN, SLOTS, D)
        for k in range(1, XN):
            x_copies.append(
                start(stage.at[slot, (x + k) % XN], buf.at[x * ZN + source], s.away_sems, (slot, k - 1), x_peers[k])
            )
        buf[x * ZN + source] = stage[slot, x]

    fill(0)
    for copy in list_copies:
        copy.wait_recv()
    lists[...] = (lists_own[x] + lists_in[0] + lists_in[1] + lists_in[2]).astype(jnp.int32)
    for step, slots in enumerate(((1, 5), (2, 6), (3, 7), (4,)), 1):
        for part in range(PARTS):
            for slot in slots:
                forward(slot, part)
        for slot in slots if step > 1 else (0,) + slots:
            relay(slot)
        fill(step)
    for index in range(2, 7):
        loads[index].wait()
    for copy in x_copies:
        copy.wait_recv()

    live_rows = counts_ref[0] * 128
    act, normed, inverse, new_edges = s.act, s.normed, s.inverse, s.new_edges
    aggregate = jnp.zeros((ND, D), F32)
    for i in range(NB):
        rows = slice(i * BM, (i + 1) * BM)
        sent_rows = nn(perm[rows, :], buf[...].reshape(EDGES, D)).astype(BF16)
        pre = slope[rows, :] + nn(sent_rows, edge_first[1])
        gate = sigmoid(pre)
        act_b = (pre * gate).astype(BF16)
        act[rows, :] = act_b
        slope[rows, :] = gate * (1.0 + pre * (1.0 - gate))
        hat, inv = normalize(nn(act_b, edge_second[...]))
        normed[rows, :] = hat
        inverse[rows, :] = inv
        live = lax.broadcasted_iota(jnp.int32, (BM, 1), 0) + i * BM < live_rows
        message = jnp.where(live, hat * vectors_ref[2:3, :], 0.0).astype(BF16)
        new_edges[rows, :] = (edges[rows, :].astype(F32) + message.astype(F32)).astype(BF16)
        aggregate = aggregate + nn(hot_back[:, rows], message)
    store_edges = pltpu.make_async_copy(new_edges, new_edges_hbm, s.store_sem.at[0])
    store_edges.start()
    aggregate = aggregate.astype(BF16)

    grads = s.grads
    node_pre = nn(h, node_first[0]) + nn(aggregate, node_first[1]) + vectors_ref[1:2, :]
    node_gate = sigmoid(node_pre)
    node_act = (node_pre * node_gate).astype(BF16)
    node_hat, node_inv = normalize(nn(node_act, node_second[...]))
    s.new_nodes[...] = (h.astype(F32) + node_hat * vectors_ref[3:4, :]).astype(BF16)
    store_nodes = pltpu.make_async_copy(s.new_nodes, new_nodes_hbm, s.store_sem.at[1])
    store_nodes.start()
    upstream = node_cot[...].astype(F32)
    node_dz = norm_backward(upstream, node_hat, node_inv, vectors_ref[3:4, :]).astype(BF16)
    node_dpre = (
        nt(node_dz, node_second[...]) * (node_gate * (1.0 + node_pre * (1.0 - node_gate)))
    ).astype(BF16)
    aggregate_cot = nt(node_dpre, node_first[1]).astype(BF16)
    col_node = jnp.sum(node_dpre.astype(F32), 0, keepdims=True)
    col_node_scale = jnp.sum(upstream * node_hat, 0, keepdims=True)
    grads[4] = tn(h, node_dpre).astype(BF16)
    grads[5] = tn(aggregate, node_dpre).astype(BF16)
    grads[6] = tn(node_act, node_dz).astype(BF16)
    s.node_part[...] = upstream + nt(node_dpre, node_first[0])

    def make(src, dst, sems, index, device):
        return remote(src, dst, sems[0].at[index], sems[1].at[index], device)

    def row_chunk(index):
        return pl.ds(pl.multiple_of(index * 128, 128), 128)

    class Share:
        def __init__(self, owner, first, count, held, final):
            t = SimpleNamespace(**held)
            self.owner, self.first, self.count, self.final = owner, first, count, final
            self.core_in, self.pair = t.core_in, t.pair
            self.a_in, self.a_sum = t.a_in, t.a_sum
            self.b_in, self.b_sum, self.z_in = t.b_in, t.b_sum, t.z_in
            columns_first = owner == 0
            if columns_first:
                self.a_place, self.b_place, a_peers, b_peers = y, x, y_peers, x_peers
                self.cuts = [(slice(None), slice(j * 128, (j + 1) * 128)) for j in range(4)]
            else:
                self.a_place, self.b_place, a_peers, b_peers = x, y, x_peers, y_peers
                self.cuts = [(slice(j * 128, (j + 1) * 128), slice(None)) for j in range(4)]

            def b_cut(k):
                piece = row_chunk((self.b_place + k) % 4)
                return (slice(None), piece, slice(None)) if columns_first else (slice(None), slice(None), piece)

            self.b_own = b_cut(0)
            self.core_copies = [
                make(grads.at[first + m], self.core_in.at[m], t.core_sems, m, partner) for m in range(count)
            ]
            self.a_copies = [
                [
                    make(self.pair.at[(self.a_place + k) % 4, m], self.a_in.at[k - 1, m], t.a_sems, (k - 1, m), a_peers[k])
                    for k in (2, 1, 3)
                ]
                for m in range(count)
            ]
            self.b_copies = [
                make(self.a_sum.at[b_cut(k)], self.b_in.at[k - 1], t.b_sems, k - 1, b_peers[k]) for k in (2, 1, 3)
            ]
            self.z_copies = [
                make(
                    self.b_sum.at[:, pl.ds(pl.multiple_of(((z + k) % ZN) * 16, 16), 16), :],
                    self.z_in.at[k - 1],
                    t.z_sems,
                    k - 1,
                    z_peers[k],
                )
                for k in (4, 3, 5, 2, 6, 1, 7)
            ]
            self.dp_copies = [
                remote(final.at[y], final.at[y], t.dp_sems[0].at[k - 1], t.dp_sems[1].at[y], dp_peers[k])
                for k in range(1, 8)
            ]
            self.dp_in = [
                remote(
                    final.at[(y + k) % YN],
                    final.at[(y + k) % YN],
                    t.dp_sems[0].at[0],
                    t.dp_sems[1].at[(y + k) % YN],
                    dp_peers[1],
                )
                for k in range(YN)
            ]

        def give(self, m):
            @pl.when(core != self.owner)
            def _():
                self.core_copies[m].start()

        def across_a(self, m):
            @pl.when(core == self.owner)
            def _():
                self.core_copies[m].wait_recv()
                for j, (rows, lanes) in enumerate(self.cuts):
                    self.pair[j, m] = (
                        grads[self.first + m, rows, lanes].astype(F32) + self.core_in[m, rows, lanes].astype(F32)
                    ).astype(BF16)
                for copy in self.a_copies[m]:
                    copy.start()

        def across_b(self):
            @pl.when(core == self.owner)
            def _():
                for m in range(self.count):
                    for copy in self.a_copies[m]:
                        copy.wait_recv()
                    self.a_sum[m] = (
                        self.pair[self.a_place, m].astype(F32)
                        + self.a_in[0, m].astype(F32)
                        + self.a_in[1, m].astype(F32)
                        + self.a_in[2, m].astype(F32)
                    ).astype(BF16)
                for copy in self.b_copies:
                    copy.start()

        def across_z(self):
            @pl.when(core == self.owner)
            def _():
                for copy in self.b_copies:
                    copy.wait_recv()
                self.b_sum[...] = (
                    self.a_sum[self.b_own].astype(F32)
                    + self.b_in[0].astype(F32)
                    + self.b_in[1].astype(F32)
                    + self.b_in[2].astype(F32)
                ).astype(BF16)
                for copy in self.z_copies:
                    copy.start()

        def across_dp(self):
            @pl.when(core == self.owner)
            def _():
                for copy in self.z_copies:
                    copy.wait_recv()
                total = self.b_sum[:, pl.ds(pl.multiple_of(z * 16, 16), 16), :].astype(F32)
                for k in range(ZN - 1):
                    total = total + self.z_in[k].astype(F32)
                self.final[y] = total.astype(BF16)
                for copy in self.dp_copies:
                    copy.start()

        def finish(self):
            for k in range(YN):
                if k:
                    self.dp_in[k].wait_recv()
                else:

                    @pl.when(core != self.owner)
                    def _():
                        self.dp_in[0].wait_recv()

        def drain(self):
            @pl.when(core != self.owner)
            def _():
                for copy in self.core_copies:
                    copy.wait_send()

            @pl.when(core == self.owner)
            def _():
                for copies in self.a_copies:
                    for copy in copies:
                        copy.wait_send()
                for copy in self.b_copies + self.z_copies + self.dp_copies:
                    copy.wait_send()

    node_share = Share(1, 4, 3, s.node_share, final_node)
    edge_share = Share(0, 0, 4, s.edge_share, final_edge)
    for m in range(3):
        node_share.give(m)

    dz, dpre = s.dz, s.dpre
    col_scale = jnp.zeros((1, D), F32)
    for i in range(NB):
        rows = slice(i * BM, (i + 1) * BM)
        live = lax.broadcasted_iota(jnp.int32, (BM, 1), 0) + i * BM < live_rows
        message_cot = jnp.where(live, edge_cot[rows, :].astype(F32) + nn(hot[rows, :], aggregate_cot), 0.0)
        hat = normed[rows, :]
        col_scale = col_scale + jnp.sum(message_cot * hat, 0, keepdims=True)
        dz[rows, :] = norm_backward(message_cot, hat, inverse[rows, :], vectors_ref[2:3, :]).astype(BF16)
        if i == 0:
            for m in range(3):
                node_share.across_a(m)
    grads[3] = tn(act[...], dz[...]).astype(BF16)
    edge_share.give(3)
    col_edge = jnp.zeros((1, D), F32)
    received = jnp.zeros((ND, D), F32)
    for i in range(NB):
        rows = slice(i * BM, (i + 1) * BM)
        dpre_b = (nt(dz[rows, :], edge_second[...]) * slope[rows, :]).astype(BF16)
        dpre[rows, :] = dpre_b
        col_edge = col_edge + jnp.sum(dpre_b.astype(F32), 0, keepdims=True)
        received = received + nn(hot_back[:, rows], dpre_b)
        if i == 0:
            edge_share.across_a(3)
    received = received.astype(BF16)
    grads[2] = tn(h, received).astype(BF16)
    edge_share.give(2)
    grads[0] = tn(edges[...], dpre[...]).astype(BF16)
    edge_share.give(0)
    back = s.back
    back[...] = nn(perm_back[...], dpre[...]).astype(BF16).reshape(GN, SLOTS, D)
    rows_in = s.rows_in
    row_copies = {}
    for j in REDUCE_ORDER:
        target = (z + REDUCE_OFFSET[j] + ZN) % ZN
        row_copies[j] = [
            start(back.at[((x + k) % XN) * ZN + target], rows_in.at[j, x], s.row_sems, (j, k - 1), x_peers[k])
            for k in range(1, XN)
        ]
    edge_share.across_a(2)
    edge_share.across_a(0)
    grads[1] = tn(buf[...].reshape(EDGES, D), back[...].reshape(EDGES, D)).astype(BF16)
    edge_share.give(1)

    sums = s.sums
    sums[0] = jnp.concatenate([col_edge, col_node, col_scale, col_node_scale, jnp.zeros((4, D), F32)], axis=0)
    dp_sums = [start(sums.at[0], s.dp_sums.at[k - 1], s.sdp_sems, k - 1, dp_peers[k]) for k in range(1, 8)]
    for j in REDUCE_ORDER:
        target = (z + REDUCE_OFFSET[j] + ZN) % ZN
        rows_in[j, x] = back[x * ZN + target]

    ring_out, ring_in = s.ring_out, s.ring_in
    ring_copies = {}

    def ring_step(j):
        target = (z + REDUCE_OFFSET[j] + ZN) % ZN
        for copy in row_copies[j]:
            copy.wait_recv()
        total = nn(onehot_rows(ND, lists[pl.ds(target, 1), :]), rows_in[j].reshape(ND, D))
        if j:
            for part in range(PARTS):
                piece = slice(part * rows_of, (part + 1) * rows_of)
                partial = total[piece]
                before = j + 1 if j in (2, 1, 6, 5) or (j == 3 and part == 0) else 4 if j == 7 and part == 1 else None
                if before:
                    ring_copies[before, part].wait_recv()
                    partial = partial + ring_in[before, piece].astype(F32)
                ring_out[j, piece] = partial.astype(BF16)
                ring_copies[j, part] = start(
                    ring_out.at[j, piece], ring_in.at[j, piece], s.back_sems, (j, part), up if j < 4 or (j == 4 and part == 0) else down
                )
            return
        for part in range(PARTS):
            ring_copies[1, part].wait_recv()
            ring_copies[5, part].wait_recv()
        total = total + ring_in[1].astype(F32) + ring_in[5].astype(F32)
        node_grad_ref[...] = (
            s.node_part[...] + nt(total.astype(BF16), edge_first[1]) + nt(received, edge_first[2])
        ).astype(BF16)

    def sum_step(parts, source, index):
        total = sums[source]
        for k in range(parts.shape[0]):
            total = total + parts[k]
        sums[index] = total

    edge_grad = s.edge_grad
    for i in range(NB):
        rows = slice(i * BM, (i + 1) * BM)
        edge_grad[rows, :] = (edge_cot[rows, :].astype(F32) + nt(dpre[rows, :], edge_first[0])).astype(BF16)
        if i == 0:
            edge_share.across_a(1)
        ring_step(REDUCE_ORDER[i])
    store_grad = pltpu.make_async_copy(edge_grad, edge_grad_hbm, s.store_sem.at[2])
    store_grad.start()
    node_share.across_b()
    for copy in dp_sums:
        copy.wait_recv()
    sum_step(s.dp_sums, 0, 1)
    x_sums = [start(sums.at[1], s.x_sums.at[k - 1], s.sx_sems, k - 1, x_peers[k]) for k in range(1, XN)]
    ring_step(3)
    ring_step(6)
    node_share.across_z()
    edge_share.across_b()
    ring_step(2)
    ring_step(5)
    node_share.across_dp()
    edge_share.across_z()
    for copy in x_sums:
        copy.wait_recv()
    sum_step(s.x_sums, 1, 2)
    z_sums = [start(sums.at[2], s.z_sums.at[k - 1], s.sz_sems, k - 1, z_peers[k]) for k in range(1, ZN)]
    ring_step(1)
    edge_share.across_dp()
    ring_step(0)
    for copy in z_sums:
        copy.wait_recv()
    sum_step(s.z_sums, 2, 3)
    sums_ref[...] = sums[3]
    store_edges.wait()
    store_nodes.wait()
    store_grad.wait()
    for copy in sent:
        copy.wait_send()
    edge_share.finish()
    node_share.finish()
    node_share.drain()
    edge_share.drain()


def scratch():
    v, dma = pltpu.VMEM, pltpu.SemaphoreType.DMA

    def pair(*size):
        return dma(size), dma(size)

    def share(count, a_shape):
        return dict(
            core_in=v((count, D, D), BF16),
            pair=v((4, count) + a_shape, BF16),
            a_in=v((3, count) + a_shape, BF16),
            a_sum=v((count,) + a_shape, BF16),
            b_in=v((3, count, 128, 128), BF16),
            b_sum=v((count, 128, 128), BF16),
            z_in=v((ZN - 1, count, 16, 128), BF16),
            core_sems=pair(count),
            a_sems=pair(3, count),
            b_sems=pair(3),
            z_sems=pair(ZN - 1),
            dp_sems=(dma((7,)), dma((YN,))),
        )

    return dict(
        edges=v((EDGES, D), BF16),
        edge_first=v((3, D, D), BF16),
        edge_second=v((D, D), BF16),
        node_first=v((2, D, D), BF16),
        node_second=v((D, D), BF16),
        node_cot=v((ND, D), BF16),
        edge_cot=v((EDGES, D), BF16),
        load_sem=dma((11,)),
        node=v((ND, D), BF16),
        senders=v((8, 128), jnp.int32),
        recv=v((8, 128), jnp.int32),
        vectors=v((4, D), F32),
        store_sem=dma((3,)),
        ring=v((ZN, ND, D), BF16),
        stage=v((ZN, XN, SLOTS, D), BF16),
        buf=v((GN, SLOTS, D), BF16),
        lists_own=v((XN, ZN, ND), F32),
        lists_in=v((XN - 1, ZN, ND), F32),
        lists=v((ZN, ND), jnp.int32),
        perm=v((EDGES, EDGES), BF16),
        perm_back=v((EDGES, EDGES), BF16),
        hot=v((EDGES, ND), BF16),
        hot_back=v((ND, EDGES), BF16),
        h_recv=v((ND, D), BF16),
        act=v((EDGES, D), BF16),
        slope=v((EDGES, D), F32),
        normed=v((EDGES, D), F32),
        inverse=v((EDGES, 1), F32),
        new_edges=v((EDGES, D), BF16),
        new_nodes=v((ND, D), BF16),
        edge_grad=v((EDGES, D), BF16),
        node_part=v((ND, D), F32),
        dz=v((EDGES, D), BF16),
        dpre=v((EDGES, D), BF16),
        back=v((GN, SLOTS, D), BF16),
        rows_in=v((ZN, XN, SLOTS, D), BF16),
        ring_out=v((ZN, ND, D), BF16),
        ring_in=v((ZN, ND, D), BF16),
        grads=v((7, D, D), BF16),
        sums=v((4, 8, D), F32),
        dp_sums=v((7, 8, D), F32),
        x_sums=v((XN - 1, 8, D), F32),
        z_sums=v((ZN - 1, 8, D), F32),
        hop_sems=pair(ZN, PARTS),
        list_sems=pair(XN - 1),
        away_sems=pair(ZN, XN - 1),
        row_sems=pair(ZN, XN - 1),
        back_sems=pair(ZN, PARTS),
        sdp_sems=pair(7),
        sx_sems=pair(XN - 1),
        sz_sems=pair(ZN - 1),
        edge_share=share(4, (D, 128)),
        node_share=share(3, (128, D)),
    )


def layer(counts, node, senders, recv, vectors, edges, edge_first, edge_second, node_first, node_second, node_cot, edge_cot):
    vmem = pl.BlockSpec(memory_space=pltpu.VMEM)
    hbm = pl.BlockSpec(memory_space=pl.ANY)
    return pl.pallas_call(
        layer_kernel,
        out_shape=(
            jax.ShapeDtypeStruct((ND, D), BF16),
            jax.ShapeDtypeStruct((EDGES, D), BF16),
            jax.ShapeDtypeStruct((EDGES, D), BF16),
            jax.ShapeDtypeStruct((ND, D), BF16),
            jax.ShapeDtypeStruct((YN, 4, 16, 128), BF16),
            jax.ShapeDtypeStruct((YN, 3, 16, 128), BF16),
            jax.ShapeDtypeStruct((8, D), F32),
        ),
        in_specs=[pl.BlockSpec(memory_space=pltpu.SMEM)] + [hbm] * 11,
        out_specs=(hbm,) * 3 + (vmem,) * 4,
        scratch_shapes=[scratch()],
        compiler_params=pltpu.CompilerParams(
            collective_id=0, has_side_effects=True, vmem_limit_bytes=VMEM_LIMIT
        ),
        name="layer",
    )(counts, node, senders, recv, vectors, edges, edge_first, edge_second, node_first, node_second, node_cot, edge_cot)


def outputs_kernel(
    nodes_in,
    edges_in,
    edge_grad_in,
    node_grad_in,
    edge_part,
    node_part,
    sums_ref,
    nodes_out,
    edges_out,
    edge_grad_out,
    node_grad_out,
    edge_first_ref,
    edge_second_ref,
    node_first_ref,
    node_second_ref,
    vectors_ref,
    edges_held,
    edge_grad_held,
    nodes_held,
    node_grad_held,
    in_sems,
    out_sems,
):
    moves = []
    for src, held, dst in (
        (edges_in, edges_held, edges_out),
        (edge_grad_in, edge_grad_held, edge_grad_out),
        (nodes_in, nodes_held, nodes_out),
        (node_grad_in, node_grad_held, node_grad_out),
    ):
        size = min(CHUNK, src.shape[0])
        for first in range(0, src.shape[0], size):
            piece, index = pl.ds(first, size), len(moves)
            moves.append(
                (
                    pltpu.make_async_copy(src.at[piece], held.at[piece], in_sems.at[index]),
                    pltpu.make_async_copy(held.at[piece], dst.at[piece], out_sems.at[index]),
                )
            )
    for fetch, _ in moves:
        fetch.start()
    for j in range(YN):
        lanes = slice(j * 128, (j + 1) * 128)
        for m in range(3):
            edge_first_ref[m, :, lanes] = edge_part[j, m].astype(F32)
        edge_second_ref[:, lanes] = edge_part[j, 3].astype(F32)
        for m in range(2):
            node_first_ref[m, :, lanes] = node_part[j, m].astype(F32)
        node_second_ref[:, lanes] = node_part[j, 2].astype(F32)
    shift = (D - lax.axis_index("graph") * 16) % D
    vectors_ref[...] = pltpu.roll(sums_ref[...], shift, 1)[0:4, 0:16]
    for fetch, store in moves:
        fetch.wait()
        store.start()
    for _, store in moves:
        store.wait()


def outputs(nodes, edges, edge_grad, node_grad, edge_part, node_part, sums):
    vmem = pl.BlockSpec(memory_space=pltpu.VMEM)
    hbm = pl.BlockSpec(memory_space=pl.ANY)
    return pl.pallas_call(
        outputs_kernel,
        out_shape=(
            jax.ShapeDtypeStruct((ND, D), BF16),
            jax.ShapeDtypeStruct((EDGES, D), BF16),
            jax.ShapeDtypeStruct((EDGES, D), BF16),
            jax.ShapeDtypeStruct((ND, D), BF16),
            jax.ShapeDtypeStruct((3, 16, D), F32),
            jax.ShapeDtypeStruct((16, D), F32),
            jax.ShapeDtypeStruct((2, 16, D), F32),
            jax.ShapeDtypeStruct((16, D), F32),
            jax.ShapeDtypeStruct((4, 16), F32),
        ),
        in_specs=[hbm] * 4 + [vmem] * 3,
        out_specs=(hbm,) * 4 + (vmem,) * 5,
        scratch_shapes=[
            pltpu.VMEM((EDGES, D), BF16),
            pltpu.VMEM((EDGES, D), BF16),
            pltpu.VMEM((ND, D), BF16),
            pltpu.VMEM((ND, D), BF16),
            pltpu.SemaphoreType.DMA((2 * EDGES // CHUNK + 2,)),
            pltpu.SemaphoreType.DMA((2 * EDGES // CHUNK + 2,)),
        ],
        compiler_params=pltpu.CompilerParams(vmem_limit_bytes=VMEM_LIMIT),
        name="outputs",
    )(nodes, edges, edge_grad, node_grad, edge_part, node_part, sums)


def body(
    node_latents,
    edge_latents,
    senders,
    receivers,
    block_counts,
    edge_first,
    edge_second,
    node_first,
    node_second,
    vectors,
    node_cotangent,
    edge_cotangent,
):
    new_nodes, new_edges, edge_grad, node_grad, edge_part, node_part, sums = layer(
        block_counts,
        node_latents[0],
        senders,
        receivers,
        vectors,
        edge_latents.reshape(EDGES, D),
        edge_first,
        edge_second,
        node_first,
        node_second,
        node_cotangent[0],
        edge_cotangent.reshape(EDGES, D),
    )
    new_nodes, new_edges, edge_grad, node_grad, grad_ef, grad_es, grad_nf, grad_ns, columns = outputs(
        new_nodes, new_edges, edge_grad, node_grad, edge_part, node_part, sums
    )
    shape = edge_latents.shape
    return (
        new_nodes[None],
        new_edges.reshape(shape),
        node_grad[None],
        edge_grad.reshape(shape),
        grad_ef,
        grad_es,
        grad_nf,
        grad_ns,
        columns,
    )


def solution(mesh):
    return jax.shard_map(
        body,
        mesh=mesh,
        in_specs=(
            P("dp", "graph", None),
            P("dp", "graph", None, None),
            P("graph", None),
            P("graph", None),
            P("graph"),
            P(),
            P(),
            P(),
            P(),
            P(),
            P("dp", "graph", None),
            P("dp", "graph", None, None),
        ),
        out_specs=(
            P("dp", "graph", None),
            P("dp", "graph", None, None),
            P("dp", "graph", None),
            P("dp", "graph", None, None),
            P(None, "graph", None),
            P("graph", None),
            P(None, "graph", None),
            P("graph", None),
            P(None, "graph"),
        ),
        check_vma=False,
    )
```

```python
from types import SimpleNamespace

import jax
import jax.numpy as jnp
from jax import lax
from jax.experimental import pallas as pl
from jax.experimental.pallas import tpu as pltpu
from jax.sharding import PartitionSpec as P

EPSILON = 1e-05
MESH = pl.DeviceIdType.MESH
F32 = jnp.float32
BF16 = jnp.bfloat16

XN, ZN, YN = 4, 8, 4
GN = XN * ZN
ND = 128
D = 512
EDGES = 1024
SLOTS = 32
BM = 512
NB = EDGES // BM
VMEM_LIMIT = 56 * 1024 * 1024

RING_ORDER = (0, 1, 5, 2, 6, 3, 7, 4)
RING_OFFSET = (0, -1, -2, -3, -4, 1, 2, 3)


def nn(left, right):
    return jnp.dot(left, right, preferred_element_type=F32)


def nt(left, right):
    return lax.dot_general(left, right, (((1,), (1,)), ((), ())), preferred_element_type=F32)


def tn(left, right):
    return lax.dot_general(left, right, (((0,), (0,)), ((), ())), preferred_element_type=F32)


def place():
    dp = lax.axis_index("dp")
    graph = lax.axis_index("graph")
    return dp, graph // ZN, graph % ZN


def remote(src, dst, send, recv, device):
    return pltpu.make_async_remote_copy(
        src_ref=src, dst_ref=dst, send_sem=send, recv_sem=recv, device_id=device, device_id_type=MESH
    )


def onehot_rows(count, row):
    index = lax.broadcasted_iota(jnp.int32, (count, row.shape[1]), 0)
    return jnp.where(index == row, 1.0, 0.0).astype(BF16)


def normalize(values):
    average = jnp.mean(values, -1, keepdims=True)
    centered = values - average
    inverse = lax.rsqrt(jnp.mean(centered * centered, -1, keepdims=True) + EPSILON)
    return centered * inverse, inverse


def norm_backward(upstream, normed, inverse, scales):
    scaled = upstream * scales
    return inverse * (
        scaled
        - jnp.mean(scaled, -1, keepdims=True)
        - normed * jnp.mean(scaled * normed, -1, keepdims=True)
    )


def sigmoid(values):
    return 0.5 + 0.5 * jnp.tanh(0.5 * values)


REDUCE_ORDER = (4, 7, 3, 6, 2, 5, 1, 0)
REDUCE_OFFSET = (0, 1, 2, 3, 4, -1, -2, -3)
PARTS = 2
CHUNK = 256
FILL = EDGES // 4


def hot_columns(column, count):
    index = lax.broadcasted_iota(jnp.int32, (column.shape[0], count), 1)
    return jnp.where(index == column, 1.0, 0.0).astype(BF16)


def columns_of(rows):
    padded = jnp.concatenate([rows.astype(F32), jnp.zeros((128 - rows.shape[0], 128), F32)], axis=0)
    return padded.T.astype(jnp.int32)


def layer_kernel(
    counts_ref,
    node_hbm,
    senders_hbm,
    recv_hbm,
    vectors_hbm,
    edge_hbm,
    edge_first_hbm,
    edge_second_hbm,
    node_first_hbm,
    node_second_hbm,
    node_cot_hbm,
    edge_cot_hbm,
    new_nodes_hbm,
    new_edges_hbm,
    edge_grad_hbm,
    node_grad_ref,
    final_edge,
    final_node,
    sums_ref,
    held,
):
    s = SimpleNamespace(**held)
    dp, x, z = place()
    graph = x * ZN + z
    y, core = dp // 2, dp % 2
    partner = (y * 2 + (1 - core), graph)
    x_peers = [None] + [(dp, ((x + k) % XN) * ZN + z) for k in range(1, XN)]
    z_peers = [None] + [(dp, x * ZN + (z + k) % ZN) for k in range(1, ZN)]
    y_peers = [None] + [(((y + k) % YN) * 2 + core, graph) for k in range(1, YN)]
    dp_peers = [None] + [((dp + k) % 8, graph) for k in range(1, 8)]
    up, down = z_peers[1], z_peers[ZN - 1]

    peers = x_peers[1:] + z_peers[1:] + dp_peers[1:]
    barrier = pltpu.get_barrier_semaphore()
    for device in peers:
        pl.semaphore_signal(barrier, inc=1, device_id=device, device_id_type=MESH)

    node_ref, senders_ref, recv_ref, vectors_ref = s.node, s.senders, s.recv, s.vectors
    loads = {}
    for index, (hbm, ref) in enumerate(
        (
            (edge_first_hbm, s.edge_first),
            (edge_hbm, s.edges),
            (edge_second_hbm, s.edge_second),
            (node_first_hbm, s.node_first),
            (node_second_hbm, s.node_second),
            (node_cot_hbm, s.node_cot),
            (edge_cot_hbm, s.edge_cot),
            (node_hbm, s.node),
            (senders_hbm, s.senders),
            (recv_hbm, s.recv),
            (vectors_hbm, s.vectors),
        )
    ):
        loads[index] = pltpu.make_async_copy(hbm, ref, s.load_sem.at[index])
    for index in (7, 8, 9, 10, 0, 1, 2, 3, 4, 5, 6):
        loads[index].start()
    edges, edge_first, edge_second = s.edges, s.edge_first, s.edge_second
    node_first, node_second = s.node_first, s.node_second
    edge_cot, node_cot = s.edge_cot, s.node_cot

    loads[7].wait()
    pl.semaphore_wait(barrier, len(peers))
    sent = []

    def start(src, dst, sems, index, device):
        copy = remote(src, dst, sems[0].at[index], sems[1].at[index], device)
        copy.start()
        sent.append(copy)
        return copy

    ring, buf = s.ring, s.buf
    rows_of = ND // PARTS

    def hop(src, slot, device, part):
        piece = pl.ds(part * rows_of, rows_of)
        return start(src.at[piece], ring.at[slot, piece], s.hop_sems, (slot, part), device)

    hops = {}
    for part in range(PARTS):
        hops[1, part] = hop(node_ref, 1, up, part)
        hops[5, part] = hop(node_ref, 5, down, part)

    for index in (8, 9, 10):
        loads[index].wait()
    senders = senders_ref[...]
    owners = senders // ND
    local = (senders % ND).astype(F32)
    earlier = jnp.where(
        lax.broadcasted_iota(jnp.int32, (ND, ND), 0) < lax.broadcasted_iota(jnp.int32, (ND, ND), 1), 1.0, 0.0
    ).astype(BF16)
    base = jnp.zeros((GN, 1), F32)
    table = jnp.zeros((GN, ND), F32)
    lane = lax.broadcasted_iota(jnp.int32, (ND, ND), 0)
    group = lax.broadcasted_iota(jnp.int32, (GN, ND), 0)
    slot_rows = []
    for b in range(EDGES // ND):
        owner = owners[b : b + 1, :]
        mine = jnp.where(group == owner, 1.0, 0.0)
        before = nn(mine.astype(BF16), earlier) + base
        rank = jnp.sum(mine * before, axis=0, keepdims=True).astype(jnp.int32)
        base = base + jnp.sum(mine, axis=1, keepdims=True)
        slot_rows.append(owner * SLOTS + rank)
        column = jnp.where(lane == rank + SLOTS * x, 1.0, 0.0).astype(BF16)
        table = table + nt((mine * local[b : b + 1, :]).astype(BF16), column)
    lists_own, lists_in, lists = s.lists_own, s.lists_in, s.lists
    lists_own[...] = table.reshape(XN, ZN, ND)
    list_copies = [
        start(lists_own.at[(x + k) % XN], lists_in.at[k - 1], s.list_sems, k - 1, x_peers[k]) for k in range(1, XN)
    ]
    slot_columns = columns_of(jnp.concatenate(slot_rows, axis=0))
    recv = recv_ref[...] - graph * ND
    recv_columns = columns_of(recv)
    perm, perm_back, hot, hot_back, slope = s.perm, s.perm_back, s.hot, s.hot_back, s.slope
    h = node_ref[...]

    def fill(step):
        if step == 0:
            loads[0].wait()
            s.h_recv[...] = nn(h, edge_first[2]).astype(BF16)
        elif step == 1:
            loads[1].wait()
        if step:
            rows = slice((step - 1) * FILL, step * FILL)
            for b in range((step - 1) * FILL // 128, step * FILL // 128):
                block = slice(b * 128, (b + 1) * 128)
                perm[block, :] = hot_columns(slot_columns[:, b : b + 1], EDGES)
                perm_back[:, block] = onehot_rows(EDGES, slot_rows[b])
                hot[block, :] = hot_columns(recv_columns[:, b : b + 1], ND)
                hot_back[:, block] = onehot_rows(ND, recv[b : b + 1, :])
            slope[rows, :] = (
                nn(edges[rows, :], edge_first[0]) + nn(hot[rows, :], s.h_recv[...]) + vectors_ref[0:1, :]
            )

    stage = s.stage
    x_copies = []

    def forward(slot, part):
        hops[slot, part].wait_recv()
        if slot in (1, 2) or (slot == 3 and part == 0):
            hops[slot + 1, part] = hop(ring.at[slot], slot + 1, up, part)
        elif slot in (5, 6):
            hops[slot + 1, part] = hop(ring.at[slot], slot + 1, down, part)
        elif slot == 7 and part == 1:
            hops[4, part] = hop(ring.at[slot], 4, down, part)

    def relay(slot):
        source = (z + RING_OFFSET[slot] + ZN) % ZN
        chosen = onehot_rows(ND, lists[pl.ds(source, 1), :])
        stage[slot] = tn(chosen, ring[slot] if slot else h).astype(BF16).reshape(XN, SLOTS, D)
        for k in range(1, XN):
            x_copies.append(
                start(stage.at[slot, (x + k) % XN], buf.at[x * ZN + source], s.away_sems, (slot, k - 1), x_peers[k])
            )
        buf[x * ZN + source] = stage[slot, x]

    fill(0)
    for copy in list_copies:
        copy.wait_recv()
    lists[...] = (lists_own[x] + lists_in[0] + lists_in[1] + lists_in[2]).astype(jnp.int32)
    for step, slots in enumerate(((1, 5), (2, 6), (3, 7), (4,)), 1):
        for part in range(PARTS):
            for slot in slots:
                forward(slot, part)
        for slot in slots if step > 1 else (0,) + slots:
            relay(slot)
        fill(step)
    for index in range(2, 7):
        loads[index].wait()
    for copy in x_copies:
        copy.wait_recv()

    live_rows = counts_ref[0] * 128
    act, normed, inverse, new_edges = s.act, s.normed, s.inverse, s.new_edges
    aggregate = jnp.zeros((ND, D), F32)
    for i in range(NB):
        rows = slice(i * BM, (i + 1) * BM)
        sent_rows = nn(perm[rows, :], buf[...].reshape(EDGES, D)).astype(BF16)
        pre = slope[rows, :] + nn(sent_rows, edge_first[1])
        gate = sigmoid(pre)
        act_b = (pre * gate).astype(BF16)
        act[rows, :] = act_b
        slope[rows, :] = gate * (1.0 + pre * (1.0 - gate))
        hat, inv = normalize(nn(act_b, edge_second[...]))
        normed[rows, :] = hat
        inverse[rows, :] = inv
        live = lax.broadcasted_iota(jnp.int32, (BM, 1), 0) + i * BM < live_rows
        message = jnp.where(live, hat * vectors_ref[2:3, :], 0.0).astype(BF16)
        new_edges[rows, :] = (edges[rows, :].astype(F32) + message.astype(F32)).astype(BF16)
        aggregate = aggregate + nn(hot_back[:, rows], message)
    store_edges = pltpu.make_async_copy(new_edges, new_edges_hbm, s.store_sem.at[0])
    store_edges.start()
    aggregate = aggregate.astype(BF16)

    grads = s.grads
    node_pre = nn(h, node_first[0]) + nn(aggregate, node_first[1]) + vectors_ref[1:2, :]
    node_gate = sigmoid(node_pre)
    node_act = (node_pre * node_gate).astype(BF16)
    node_hat, node_inv = normalize(nn(node_act, node_second[...]))
    s.new_nodes[...] = (h.astype(F32) + node_hat * vectors_ref[3:4, :]).astype(BF16)
    store_nodes = pltpu.make_async_copy(s.new_nodes, new_nodes_hbm, s.store_sem.at[1])
    store_nodes.start()
    upstream = node_cot[...].astype(F32)
    node_dz = norm_backward(upstream, node_hat, node_inv, vectors_ref[3:4, :]).astype(BF16)
    node_dpre = (
        nt(node_dz, node_second[...]) * (node_gate * (1.0 + node_pre * (1.0 - node_gate)))
    ).astype(BF16)
    aggregate_cot = nt(node_dpre, node_first[1]).astype(BF16)
    col_node = jnp.sum(node_dpre.astype(F32), 0, keepdims=True)
    col_node_scale = jnp.sum(upstream * node_hat, 0, keepdims=True)
    grads[4] = tn(h, node_dpre).astype(BF16)
    grads[5] = tn(aggregate, node_dpre).astype(BF16)
    grads[6] = tn(node_act, node_dz).astype(BF16)
    s.node_part[...] = upstream + nt(node_dpre, node_first[0])

    def make(src, dst, sems, index, device):
        return remote(src, dst, sems[0].at[index], sems[1].at[index], device)

    def row_chunk(index):
        return pl.ds(pl.multiple_of(index * 128, 128), 128)

    class Share:
        def __init__(self, owner, first, count, held, final):
            t = SimpleNamespace(**held)
            self.owner, self.first, self.count, self.final = owner, first, count, final
            self.core_in, self.pair = t.core_in, t.pair
            self.a_in, self.a_sum = t.a_in, t.a_sum
            self.b_in, self.b_sum, self.z_in = t.b_in, t.b_sum, t.z_in
            columns_first = owner == 0
            if columns_first:
                self.a_place, self.b_place, a_peers, b_peers = y, x, y_peers, x_peers
                self.cuts = [(slice(None), slice(j * 128, (j + 1) * 128)) for j in range(4)]
            else:
                self.a_place, self.b_place, a_peers, b_peers = x, y, x_peers, y_peers
                self.cuts = [(slice(j * 128, (j + 1) * 128), slice(None)) for j in range(4)]

            def b_cut(k):
                piece = row_chunk((self.b_place + k) % 4)
                return (slice(None), piece, slice(None)) if columns_first else (slice(None), slice(None), piece)

            self.b_own = b_cut(0)
            self.core_copies = [
                make(grads.at[first + m], self.core_in.at[m], t.core_sems, m, partner) for m in range(count)
            ]
            self.a_copies = [
                [
                    make(self.pair.at[(self.a_place + k) % 4, m], self.a_in.at[k - 1, m], t.a_sems, (k - 1, m), a_peers[k])
                    for k in (2, 1, 3)
                ]
                for m in range(count)
            ]
            self.b_copies = [
                make(self.a_sum.at[b_cut(k)], self.b_in.at[k - 1], t.b_sems, k - 1, b_peers[k]) for k in (2, 1, 3)
            ]
            self.z_copies = [
                make(
                    self.b_sum.at[:, pl.ds(pl.multiple_of(((z + k) % ZN) * 16, 16), 16), :],
                    self.z_in.at[k - 1],
                    t.z_sems,
                    k - 1,
                    z_peers[k],
                )
                for k in (4, 3, 5, 2, 6, 1, 7)
            ]
            self.dp_copies = [
                remote(final.at[y], final.at[y], t.dp_sems[0].at[k - 1], t.dp_sems[1].at[y], dp_peers[k])
                for k in range(1, 8)
            ]
            self.dp_in = [
                remote(
                    final.at[(y + k) % YN],
                    final.at[(y + k) % YN],
                    t.dp_sems[0].at[0],
                    t.dp_sems[1].at[(y + k) % YN],
                    dp_peers[1],
                )
                for k in range(YN)
            ]

        def give(self, m):
            @pl.when(core != self.owner)
            def _():
                self.core_copies[m].start()

        def across_a(self, m):
            @pl.when(core == self.owner)
            def _():
                self.core_copies[m].wait_recv()
                for j, (rows, lanes) in enumerate(self.cuts):
                    self.pair[j, m] = (
                        grads[self.first + m, rows, lanes].astype(F32) + self.core_in[m, rows, lanes].astype(F32)
                    ).astype(BF16)
                for copy in self.a_copies[m]:
                    copy.start()

        def across_b(self):
            @pl.when(core == self.owner)
            def _():
                for m in range(self.count):
                    for copy in self.a_copies[m]:
                        copy.wait_recv()
                    self.a_sum[m] = (
                        self.pair[self.a_place, m].astype(F32)
                        + self.a_in[0, m].astype(F32)
                        + self.a_in[1, m].astype(F32)
                        + self.a_in[2, m].astype(F32)
                    ).astype(BF16)
                for copy in self.b_copies:
                    copy.start()

        def across_z(self):
            @pl.when(core == self.owner)
            def _():
                for copy in self.b_copies:
                    copy.wait_recv()
                self.b_sum[...] = (
                    self.a_sum[self.b_own].astype(F32)
                    + self.b_in[0].astype(F32)
                    + self.b_in[1].astype(F32)
                    + self.b_in[2].astype(F32)
                ).astype(BF16)
                for copy in self.z_copies:
                    copy.start()

        def across_dp(self):
            @pl.when(core == self.owner)
            def _():
                for copy in self.z_copies:
                    copy.wait_recv()
                total = self.b_sum[:, pl.ds(pl.multiple_of(z * 16, 16), 16), :].astype(F32)
                for k in range(ZN - 1):
                    total = total + self.z_in[k].astype(F32)
                self.final[y] = total.astype(BF16)
                for copy in self.dp_copies:
                    copy.start()

        def finish(self):
            for k in range(YN):
                if k:
                    self.dp_in[k].wait_recv()
                else:

                    @pl.when(core != self.owner)
                    def _():
                        self.dp_in[0].wait_recv()

        def drain(self):
            @pl.when(core != self.owner)
            def _():
                for copy in self.core_copies:
                    copy.wait_send()

            @pl.when(core == self.owner)
            def _():
                for copies in self.a_copies:
                    for copy in copies:
                        copy.wait_send()
                for copy in self.b_copies + self.z_copies + self.dp_copies:
                    copy.wait_send()

    node_share = Share(1, 4, 3, s.node_share, final_node)
    edge_share = Share(0, 0, 4, s.edge_share, final_edge)
    for m in range(3):
        node_share.give(m)

    dz, dpre = s.dz, s.dpre
    col_scale = jnp.zeros((1, D), F32)
    for i in range(NB):
        rows = slice(i * BM, (i + 1) * BM)
        live = lax.broadcasted_iota(jnp.int32, (BM, 1), 0) + i * BM < live_rows
        message_cot = jnp.where(live, edge_cot[rows, :].astype(F32) + nn(hot[rows, :], aggregate_cot), 0.0)
        hat = normed[rows, :]
        col_scale = col_scale + jnp.sum(message_cot * hat, 0, keepdims=True)
        dz[rows, :] = norm_backward(message_cot, hat, inverse[rows, :], vectors_ref[2:3, :]).astype(BF16)
        if i == 0:
            for m in range(3):
                node_share.across_a(m)
    grads[3] = tn(act[...], dz[...]).astype(BF16)
    edge_share.give(3)
    col_edge = jnp.zeros((1, D), F32)
    received = jnp.zeros((ND, D), F32)
    for i in range(NB):
        rows = slice(i * BM, (i + 1) * BM)
        dpre_b = (nt(dz[rows, :], edge_second[...]) * slope[rows, :]).astype(BF16)
        dpre[rows, :] = dpre_b
        col_edge = col_edge + jnp.sum(dpre_b.astype(F32), 0, keepdims=True)
        received = received + nn(hot_back[:, rows], dpre_b)
        if i == 0:
            edge_share.across_a(3)
    received = received.astype(BF16)
    back = s.back
    back[...] = nn(perm_back[...], dpre[...]).astype(BF16).reshape(GN, SLOTS, D)
    rows_in = s.rows_in
    row_copies = {}
    for j in REDUCE_ORDER:
        target = (z + REDUCE_OFFSET[j] + ZN) % ZN
        row_copies[j] = [
            start(back.at[((x + k) % XN) * ZN + target], rows_in.at[j, x], s.row_sems, (j, k - 1), x_peers[k])
            for k in range(1, XN)
        ]
    grads[2] = tn(h, received).astype(BF16)
    edge_share.give(2)
    grads[0] = tn(edges[...], dpre[...]).astype(BF16)
    edge_share.give(0)
    edge_share.across_a(2)
    edge_share.across_a(0)
    grads[1] = tn(buf[...].reshape(EDGES, D), back[...].reshape(EDGES, D)).astype(BF16)
    edge_share.give(1)

    sums = s.sums
    sums[0] = jnp.concatenate([col_edge, col_node, col_scale, col_node_scale, jnp.zeros((4, D), F32)], axis=0)
    dp_sums = [start(sums.at[0], s.dp_sums.at[k - 1], s.sdp_sems, k - 1, dp_peers[k]) for k in range(1, 8)]
    for j in REDUCE_ORDER:
        target = (z + REDUCE_OFFSET[j] + ZN) % ZN
        rows_in[j, x] = back[x * ZN + target]

    ring_out, ring_in = s.ring_out, s.ring_in
    ring_copies = {}

    def ring_step(j):
        target = (z + REDUCE_OFFSET[j] + ZN) % ZN
        for copy in row_copies[j]:
            copy.wait_recv()
        total = nn(onehot_rows(ND, lists[pl.ds(target, 1), :]), rows_in[j].reshape(ND, D))
        if j:
            for part in range(PARTS):
                piece = slice(part * rows_of, (part + 1) * rows_of)
                partial = total[piece]
                before = j + 1 if j in (2, 1, 6, 5) or (j == 3 and part == 0) else 4 if j == 7 and part == 1 else None
                if before:
                    ring_copies[before, part].wait_recv()
                    partial = partial + ring_in[before, piece].astype(F32)
                ring_out[j, piece] = partial.astype(BF16)
                ring_copies[j, part] = start(
                    ring_out.at[j, piece], ring_in.at[j, piece], s.back_sems, (j, part), up if j < 4 or (j == 4 and part == 0) else down
                )
            return
        for part in range(PARTS):
            ring_copies[1, part].wait_recv()
            ring_copies[5, part].wait_recv()
        total = total + ring_in[1].astype(F32) + ring_in[5].astype(F32)
        node_grad_ref[...] = (
            s.node_part[...] + nt(total.astype(BF16), edge_first[1]) + nt(received, edge_first[2])
        ).astype(BF16)

    def sum_step(parts, source, index):
        total = sums[source]
        for k in range(parts.shape[0]):
            total = total + parts[k]
        sums[index] = total

    edge_grad = s.edge_grad
    for i in range(NB):
        rows = slice(i * BM, (i + 1) * BM)
        edge_grad[rows, :] = (edge_cot[rows, :].astype(F32) + nt(dpre[rows, :], edge_first[0])).astype(BF16)
        if i == 0:
            edge_share.across_a(1)
        ring_step(REDUCE_ORDER[i])
    store_grad = pltpu.make_async_copy(edge_grad, edge_grad_hbm, s.store_sem.at[2])
    store_grad.start()
    node_share.across_b()
    for copy in dp_sums:
        copy.wait_recv()
    sum_step(s.dp_sums, 0, 1)
    x_sums = [start(sums.at[1], s.x_sums.at[k - 1], s.sx_sems, k - 1, x_peers[k]) for k in range(1, XN)]
    ring_step(3)
    ring_step(6)
    node_share.across_z()
    edge_share.across_b()
    ring_step(2)
    ring_step(5)
    node_share.across_dp()
    edge_share.across_z()
    for copy in x_sums:
        copy.wait_recv()
    sum_step(s.x_sums, 1, 2)
    z_sums = [start(sums.at[2], s.z_sums.at[k - 1], s.sz_sems, k - 1, z_peers[k]) for k in range(1, ZN)]
    ring_step(1)
    edge_share.across_dp()
    ring_step(0)
    for copy in z_sums:
        copy.wait_recv()
    sum_step(s.z_sums, 2, 3)
    sums_ref[...] = sums[3]
    store_edges.wait()
    store_nodes.wait()
    store_grad.wait()
    for copy in sent:
        copy.wait_send()
    edge_share.finish()
    node_share.finish()
    node_share.drain()
    edge_share.drain()


def scratch():
    v, dma = pltpu.VMEM, pltpu.SemaphoreType.DMA

    def pair(*size):
        return dma(size), dma(size)

    def share(count, a_shape):
        return dict(
            core_in=v((count, D, D), BF16),
            pair=v((4, count) + a_shape, BF16),
            a_in=v((3, count) + a_shape, BF16),
            a_sum=v((count,) + a_shape, BF16),
            b_in=v((3, count, 128, 128), BF16),
            b_sum=v((count, 128, 128), BF16),
            z_in=v((ZN - 1, count, 16, 128), BF16),
            core_sems=pair(count),
            a_sems=pair(3, count),
            b_sems=pair(3),
            z_sems=pair(ZN - 1),
            dp_sems=(dma((7,)), dma((YN,))),
        )

    return dict(
        edges=v((EDGES, D), BF16),
        edge_first=v((3, D, D), BF16),
        edge_second=v((D, D), BF16),
        node_first=v((2, D, D), BF16),
        node_second=v((D, D), BF16),
        node_cot=v((ND, D), BF16),
        edge_cot=v((EDGES, D), BF16),
        load_sem=dma((11,)),
        node=v((ND, D), BF16),
        senders=v((8, 128), jnp.int32),
        recv=v((8, 128), jnp.int32),
        vectors=v((4, D), F32),
        store_sem=dma((3,)),
        ring=v((ZN, ND, D), BF16),
        stage=v((ZN, XN, SLOTS, D), BF16),
        buf=v((GN, SLOTS, D), BF16),
        lists_own=v((XN, ZN, ND), F32),
        lists_in=v((XN - 1, ZN, ND), F32),
        lists=v((ZN, ND), jnp.int32),
        perm=v((EDGES, EDGES), BF16),
        perm_back=v((EDGES, EDGES), BF16),
        hot=v((EDGES, ND), BF16),
        hot_back=v((ND, EDGES), BF16),
        h_recv=v((ND, D), BF16),
        act=v((EDGES, D), BF16),
        slope=v((EDGES, D), F32),
        normed=v((EDGES, D), F32),
        inverse=v((EDGES, 1), F32),
        new_edges=v((EDGES, D), BF16),
        new_nodes=v((ND, D), BF16),
        edge_grad=v((EDGES, D), BF16),
        node_part=v((ND, D), F32),
        dz=v((EDGES, D), BF16),
        dpre=v((EDGES, D), BF16),
        back=v((GN, SLOTS, D), BF16),
        rows_in=v((ZN, XN, SLOTS, D), BF16),
        ring_out=v((ZN, ND, D), BF16),
        ring_in=v((ZN, ND, D), BF16),
        grads=v((7, D, D), BF16),
        sums=v((4, 8, D), F32),
        dp_sums=v((7, 8, D), F32),
        x_sums=v((XN - 1, 8, D), F32),
        z_sums=v((ZN - 1, 8, D), F32),
        hop_sems=pair(ZN, PARTS),
        list_sems=pair(XN - 1),
        away_sems=pair(ZN, XN - 1),
        row_sems=pair(ZN, XN - 1),
        back_sems=pair(ZN, PARTS),
        sdp_sems=pair(7),
        sx_sems=pair(XN - 1),
        sz_sems=pair(ZN - 1),
        edge_share=share(4, (D, 128)),
        node_share=share(3, (128, D)),
    )


def layer(counts, node, senders, recv, vectors, edges, edge_first, edge_second, node_first, node_second, node_cot, edge_cot):
    vmem = pl.BlockSpec(memory_space=pltpu.VMEM)
    hbm = pl.BlockSpec(memory_space=pl.ANY)
    return pl.pallas_call(
        layer_kernel,
        out_shape=(
            jax.ShapeDtypeStruct((ND, D), BF16),
            jax.ShapeDtypeStruct((EDGES, D), BF16),
            jax.ShapeDtypeStruct((EDGES, D), BF16),
            jax.ShapeDtypeStruct((ND, D), BF16),
            jax.ShapeDtypeStruct((YN, 4, 16, 128), BF16),
            jax.ShapeDtypeStruct((YN, 3, 16, 128), BF16),
            jax.ShapeDtypeStruct((8, D), F32),
        ),
        in_specs=[pl.BlockSpec(memory_space=pltpu.SMEM)] + [hbm] * 11,
        out_specs=(hbm,) * 3 + (vmem,) * 4,
        scratch_shapes=[scratch()],
        compiler_params=pltpu.CompilerParams(
            collective_id=0, has_side_effects=True, vmem_limit_bytes=VMEM_LIMIT
        ),
        name="layer",
    )(counts, node, senders, recv, vectors, edges, edge_first, edge_second, node_first, node_second, node_cot, edge_cot)


def outputs_kernel(*refs):
    copied_in, parts_in, copied_out, small_out = refs[0:4], refs[4:7], refs[7:11], refs[11:16]
    copied, parts, small = refs[16:20], refs[20:23], refs[23:28]
    in_sems, out_sems, part_sems, small_sems = refs[28:32]
    moves = []
    for src, held, dst in zip(copied_in, copied, copied_out):
        size = min(CHUNK, src.shape[0])
        for first in range(0, src.shape[0], size):
            piece, index = pl.ds(first, size), len(moves)
            moves.append(
                (
                    pltpu.make_async_copy(src.at[piece], held.at[piece], in_sems.at[index]),
                    pltpu.make_async_copy(held.at[piece], dst.at[piece], out_sems.at[index]),
                )
            )
    loads = [pltpu.make_async_copy(src, held, part_sems.at[i]) for i, (src, held) in enumerate(zip(parts_in, parts))]
    stores = [pltpu.make_async_copy(held, dst, small_sems.at[i]) for i, (held, dst) in enumerate(zip(small, small_out))]
    for load in loads:
        load.start()
    for fetch, _ in moves:
        fetch.start()
    for load in loads:
        load.wait()
    edge_part, node_part, sums_ref = parts
    edge_first_ref, edge_second_ref, node_first_ref, node_second_ref, vectors_ref = small
    for j in range(YN):
        lanes = slice(j * 128, (j + 1) * 128)
        for m in range(3):
            edge_first_ref[m, :, lanes] = edge_part[j, m].astype(F32)
        edge_second_ref[:, lanes] = edge_part[j, 3].astype(F32)
        for m in range(2):
            node_first_ref[m, :, lanes] = node_part[j, m].astype(F32)
        node_second_ref[:, lanes] = node_part[j, 2].astype(F32)
    shift = (D - lax.axis_index("graph") * 16) % D
    vectors_ref[...] = pltpu.roll(sums_ref[...], shift, 1)[0:4, 0:16]
    for store in stores:
        store.start()
    for fetch, store in moves:
        fetch.wait()
        store.start()
    for _, store in moves:
        store.wait()
    for store in stores:
        store.wait()


def outputs(nodes, edges, edge_grad, node_grad, edge_part, node_part, sums):
    hbm = pl.BlockSpec(memory_space=pl.ANY)
    copied = [((EDGES, D), BF16), ((EDGES, D), BF16), ((ND, D), BF16), ((ND, D), BF16)]
    parts = [((YN, 4, 16, 128), BF16), ((YN, 3, 16, 128), BF16), ((8, D), F32)]
    small = [((3, 16, D), F32), ((16, D), F32), ((2, 16, D), F32), ((16, D), F32), ((4, 16), F32)]
    moves = 2 * EDGES // CHUNK + 2
    new_edges, edge_grad, new_nodes, node_grad, *rest = pl.pallas_call(
        outputs_kernel,
        out_shape=tuple(jax.ShapeDtypeStruct(*one) for one in copied + small),
        in_specs=[hbm] * 7,
        out_specs=(hbm,) * 9,
        scratch_shapes=[pltpu.VMEM(*one) for one in copied + parts + small]
        + [pltpu.SemaphoreType.DMA((count,)) for count in (moves, moves, 3, 5)],
        compiler_params=pltpu.CompilerParams(vmem_limit_bytes=VMEM_LIMIT),
        name="outputs",
    )(edges, edge_grad, nodes, node_grad, edge_part, node_part, sums)
    return new_nodes, new_edges, edge_grad, node_grad, *rest


def body(
    node_latents,
    edge_latents,
    senders,
    receivers,
    block_counts,
    edge_first,
    edge_second,
    node_first,
    node_second,
    vectors,
    node_cotangent,
    edge_cotangent,
):
    new_nodes, new_edges, edge_grad, node_grad, edge_part, node_part, sums = layer(
        block_counts,
        node_latents[0],
        senders,
        receivers,
        vectors,
        edge_latents.reshape(EDGES, D),
        edge_first,
        edge_second,
        node_first,
        node_second,
        node_cotangent[0],
        edge_cotangent.reshape(EDGES, D),
    )
    new_nodes, new_edges, edge_grad, node_grad, grad_ef, grad_es, grad_nf, grad_ns, columns = outputs(
        new_nodes, new_edges, edge_grad, node_grad, edge_part, node_part, sums
    )
    shape = edge_latents.shape
    return (
        new_nodes[None],
        new_edges.reshape(shape),
        node_grad[None],
        edge_grad.reshape(shape),
        grad_ef,
        grad_es,
        grad_nf,
        grad_ns,
        columns,
    )


def solution(mesh):
    return jax.shard_map(
        body,
        mesh=mesh,
        in_specs=(
            P("dp", "graph", None),
            P("dp", "graph", None, None),
            P("graph", None),
            P("graph", None),
            P("graph"),
            P(),
            P(),
            P(),
            P(),
            P(),
            P("dp", "graph", None),
            P("dp", "graph", None, None),
        ),
        out_specs=(
            P("dp", "graph", None),
            P("dp", "graph", None, None),
            P("dp", "graph", None),
            P("dp", "graph", None, None),
            P(None, "graph", None),
            P("graph", None),
            P(None, "graph", None),
            P("graph", None),
            P(None, "graph"),
        ),
        check_vma=False,
    )
```

```python
from types import SimpleNamespace

import jax
import jax.numpy as jnp
from jax import lax
from jax.experimental import pallas as pl
from jax.experimental.pallas import tpu as pltpu
from jax.sharding import PartitionSpec as P

EPSILON = 1e-05
MESH = pl.DeviceIdType.MESH
F32 = jnp.float32
BF16 = jnp.bfloat16

XN, ZN, YN = 4, 8, 4
GN = XN * ZN
ND = 128
D = 512
EDGES = 1024
SLOTS = 32
BM = 512
NB = EDGES // BM
VMEM_LIMIT = 56 * 1024 * 1024

RING_ORDER = (0, 1, 5, 2, 6, 3, 7, 4)
RING_OFFSET = (0, -1, -2, -3, -4, 1, 2, 3)


def nn(left, right):
    return jnp.dot(left, right, preferred_element_type=F32)


def nt(left, right):
    return lax.dot_general(left, right, (((1,), (1,)), ((), ())), preferred_element_type=F32)


def tn(left, right):
    return lax.dot_general(left, right, (((0,), (0,)), ((), ())), preferred_element_type=F32)


def place():
    dp = lax.axis_index("dp")
    graph = lax.axis_index("graph")
    return dp, graph // ZN, graph % ZN


def remote(src, dst, send, recv, device):
    return pltpu.make_async_remote_copy(
        src_ref=src, dst_ref=dst, send_sem=send, recv_sem=recv, device_id=device, device_id_type=MESH
    )


def onehot_rows(count, row):
    index = lax.broadcasted_iota(jnp.int32, (count, row.shape[1]), 0)
    return jnp.where(index == row, 1.0, 0.0).astype(BF16)


def normalize(values):
    average = jnp.mean(values, -1, keepdims=True)
    centered = values - average
    inverse = lax.rsqrt(jnp.mean(centered * centered, -1, keepdims=True) + EPSILON)
    return centered * inverse, inverse


def norm_backward(upstream, normed, inverse, scales):
    scaled = upstream * scales
    return inverse * (
        scaled
        - jnp.mean(scaled, -1, keepdims=True)
        - normed * jnp.mean(scaled * normed, -1, keepdims=True)
    )


def sigmoid(values):
    return 0.5 + 0.5 * jnp.tanh(0.5 * values)


REDUCE_ORDER = (4, 7, 3, 6, 2, 5, 1, 0)
REDUCE_OFFSET = (0, 1, 2, 3, 4, -1, -2, -3)
PARTS = 2
CHUNK = 256
FILL = EDGES // 4


def hot_columns(column, count):
    index = lax.broadcasted_iota(jnp.int32, (column.shape[0], count), 1)
    return jnp.where(index == column, 1.0, 0.0).astype(BF16)


def columns_of(rows):
    padded = jnp.concatenate([rows.astype(F32), jnp.zeros((128 - rows.shape[0], 128), F32)], axis=0)
    return padded.T.astype(jnp.int32)


def layer_kernel(
    counts_ref,
    node_hbm,
    senders_hbm,
    recv_hbm,
    vectors_hbm,
    edge_hbm,
    edge_first_hbm,
    edge_second_hbm,
    node_first_hbm,
    node_second_hbm,
    node_cot_hbm,
    edge_cot_hbm,
    new_nodes_hbm,
    new_edges_hbm,
    edge_grad_hbm,
    node_grad_ref,
    final_edge,
    final_node,
    sums_ref,
    held,
):
    s = SimpleNamespace(**held)
    dp, x, z = place()
    graph = x * ZN + z
    y, core = dp // 2, dp % 2
    partner = (y * 2 + (1 - core), graph)
    x_peers = [None] + [(dp, ((x + k) % XN) * ZN + z) for k in range(1, XN)]
    z_peers = [None] + [(dp, x * ZN + (z + k) % ZN) for k in range(1, ZN)]
    y_peers = [None] + [(((y + k) % YN) * 2 + core, graph) for k in range(1, YN)]
    dp_peers = [None] + [((dp + k) % 8, graph) for k in range(1, 8)]
    up, down = z_peers[1], z_peers[ZN - 1]

    peers = x_peers[1:] + z_peers[1:] + dp_peers[1:]
    barrier = pltpu.get_barrier_semaphore()
    for device in peers:
        pl.semaphore_signal(barrier, inc=1, device_id=device, device_id_type=MESH)

    node_ref, senders_ref, recv_ref, vectors_ref = s.node, s.senders, s.recv, s.vectors
    loads = {}
    for index, (hbm, ref) in enumerate(
        (
            (edge_first_hbm, s.edge_first),
            (edge_hbm, s.edges),
            (edge_second_hbm, s.edge_second),
            (node_first_hbm, s.node_first),
            (node_second_hbm, s.node_second),
            (node_cot_hbm, s.node_cot),
            (edge_cot_hbm, s.edge_cot),
            (node_hbm, s.node),
            (senders_hbm, s.senders),
            (recv_hbm, s.recv),
            (vectors_hbm, s.vectors),
        )
    ):
        loads[index] = pltpu.make_async_copy(hbm, ref, s.load_sem.at[index])
    for index in (7, 8, 9, 10, 0, 1, 2, 3, 4, 5, 6):
        loads[index].start()
    edges, edge_first, edge_second = s.edges, s.edge_first, s.edge_second
    node_first, node_second = s.node_first, s.node_second
    edge_cot, node_cot = s.edge_cot, s.node_cot

    loads[7].wait()
    pl.semaphore_wait(barrier, len(peers))
    sent = []

    def start(src, dst, sems, index, device):
        copy = remote(src, dst, sems[0].at[index], sems[1].at[index], device)
        copy.start()
        sent.append(copy)
        return copy

    ring, buf = s.ring, s.buf
    rows_of = ND // PARTS

    def hop(src, slot, device, part):
        piece = pl.ds(part * rows_of, rows_of)
        return start(src.at[piece], ring.at[slot, piece], s.hop_sems, (slot, part), device)

    hops = {}
    for part in range(PARTS):
        hops[1, part] = hop(node_ref, 1, up, part)
        hops[5, part] = hop(node_ref, 5, down, part)

    for index in (8, 9, 10):
        loads[index].wait()
    senders = senders_ref[...]
    owners = senders // ND
    local = (senders % ND).astype(F32)
    earlier = jnp.where(
        lax.broadcasted_iota(jnp.int32, (ND, ND), 0) < lax.broadcasted_iota(jnp.int32, (ND, ND), 1), 1.0, 0.0
    ).astype(BF16)
    base = jnp.zeros((GN, 1), F32)
    table = jnp.zeros((GN, ND), F32)
    lane = lax.broadcasted_iota(jnp.int32, (ND, ND), 0)
    group = lax.broadcasted_iota(jnp.int32, (GN, ND), 0)
    slot_rows = []
    for b in range(EDGES // ND):
        owner = owners[b : b + 1, :]
        mine = jnp.where(group == owner, 1.0, 0.0)
        before = nn(mine.astype(BF16), earlier) + base
        rank = jnp.sum(mine * before, axis=0, keepdims=True).astype(jnp.int32)
        base = base + jnp.sum(mine, axis=1, keepdims=True)
        slot_rows.append(owner * SLOTS + rank)
        column = jnp.where(lane == rank + SLOTS * x, 1.0, 0.0).astype(BF16)
        table = table + nt((mine * local[b : b + 1, :]).astype(BF16), column)
    lists_own, lists_in, lists = s.lists_own, s.lists_in, s.lists
    lists_own[...] = table.reshape(XN, ZN, ND)
    list_copies = [
        start(lists_own.at[(x + k) % XN], lists_in.at[k - 1], s.list_sems, k - 1, x_peers[k]) for k in range(1, XN)
    ]
    slot_columns = columns_of(jnp.concatenate(slot_rows, axis=0))
    recv = recv_ref[...] - graph * ND
    recv_columns = columns_of(recv)
    perm, perm_back, hot, hot_back, slope = s.perm, s.perm_back, s.hot, s.hot_back, s.slope
    h = node_ref[...]

    def fill(step):
        if step == 0:
            loads[0].wait()
            s.h_recv[...] = nn(h, edge_first[2]).astype(BF16)
        elif step == 1:
            loads[1].wait()
        if step:
            rows = slice((step - 1) * FILL, step * FILL)
            for b in range((step - 1) * FILL // 128, step * FILL // 128):
                block = slice(b * 128, (b + 1) * 128)
                perm[block, :] = hot_columns(slot_columns[:, b : b + 1], EDGES)
                perm_back[:, block] = onehot_rows(EDGES, slot_rows[b])
                hot[block, :] = hot_columns(recv_columns[:, b : b + 1], ND)
                hot_back[:, block] = onehot_rows(ND, recv[b : b + 1, :])
            slope[rows, :] = (
                nn(edges[rows, :], edge_first[0]) + nn(hot[rows, :], s.h_recv[...]) + vectors_ref[0:1, :]
            )

    stage = s.stage
    x_copies = []

    def forward(slot, part):
        hops[slot, part].wait_recv()
        if slot in (1, 2) or (slot == 3 and part == 0):
            hops[slot + 1, part] = hop(ring.at[slot], slot + 1, up, part)
        elif slot in (5, 6):
            hops[slot + 1, part] = hop(ring.at[slot], slot + 1, down, part)
        elif slot == 7 and part == 1:
            hops[4, part] = hop(ring.at[slot], 4, down, part)

    def relay(slot):
        source = (z + RING_OFFSET[slot] + ZN) % ZN
        chosen = onehot_rows(ND, lists[pl.ds(source, 1), :])
        stage[slot] = tn(chosen, ring[slot] if slot else h).astype(BF16).reshape(XN, SLOTS, D)
        for k in range(1, XN):
            x_copies.append(
                start(stage.at[slot, (x + k) % XN], buf.at[x * ZN + source], s.away_sems, (slot, k - 1), x_peers[k])
            )
        buf[x * ZN + source] = stage[slot, x]

    fill(0)
    for copy in list_copies:
        copy.wait_recv()
    lists[...] = (lists_own[x] + lists_in[0] + lists_in[1] + lists_in[2]).astype(jnp.int32)
    for step, slots in enumerate(((1, 5), (2, 6), (3, 7), (4,)), 1):
        for part in range(PARTS):
            for slot in slots:
                forward(slot, part)
        for slot in slots if step > 1 else (0,) + slots:
            relay(slot)
        fill(step)
    for index in range(2, 7):
        loads[index].wait()
    for copy in x_copies:
        copy.wait_recv()

    live_rows = counts_ref[0] * 128
    act, normed, inverse, new_edges = s.act, s.normed, s.inverse, s.new_edges
    aggregate = jnp.zeros((ND, D), F32)
    for i in range(NB):
        rows = slice(i * BM, (i + 1) * BM)
        sent_rows = nn(perm[rows, :], buf[...].reshape(EDGES, D)).astype(BF16)
        pre = slope[rows, :] + nn(sent_rows, edge_first[1])
        gate = sigmoid(pre)
        act_b = (pre * gate).astype(BF16)
        act[rows, :] = act_b
        slope[rows, :] = gate * (1.0 + pre * (1.0 - gate))
        hat, inv = normalize(nn(act_b, edge_second[...]))
        normed[rows, :] = hat
        inverse[rows, :] = inv
        live = lax.broadcasted_iota(jnp.int32, (BM, 1), 0) + i * BM < live_rows
        message = jnp.where(live, hat * vectors_ref[2:3, :], 0.0).astype(BF16)
        new_edges[rows, :] = (edges[rows, :].astype(F32) + message.astype(F32)).astype(BF16)
        aggregate = aggregate + nn(hot_back[:, rows], message)
    store_edges = pltpu.make_async_copy(new_edges, new_edges_hbm, s.store_sem.at[0])
    store_edges.start()
    aggregate = aggregate.astype(BF16)

    grads = s.grads
    node_pre = nn(h, node_first[0]) + nn(aggregate, node_first[1]) + vectors_ref[1:2, :]
    node_gate = sigmoid(node_pre)
    node_act = (node_pre * node_gate).astype(BF16)
    node_hat, node_inv = normalize(nn(node_act, node_second[...]))
    s.new_nodes[...] = (h.astype(F32) + node_hat * vectors_ref[3:4, :]).astype(BF16)
    store_nodes = pltpu.make_async_copy(s.new_nodes, new_nodes_hbm, s.store_sem.at[1])
    store_nodes.start()
    upstream = node_cot[...].astype(F32)
    node_dz = norm_backward(upstream, node_hat, node_inv, vectors_ref[3:4, :]).astype(BF16)
    node_dpre = (
        nt(node_dz, node_second[...]) * (node_gate * (1.0 + node_pre * (1.0 - node_gate)))
    ).astype(BF16)
    aggregate_cot = nt(node_dpre, node_first[1]).astype(BF16)
    col_node = jnp.sum(node_dpre.astype(F32), 0, keepdims=True)
    col_node_scale = jnp.sum(upstream * node_hat, 0, keepdims=True)
    grads[4] = tn(h, node_dpre).astype(BF16)
    grads[5] = tn(aggregate, node_dpre).astype(BF16)
    grads[6] = tn(node_act, node_dz).astype(BF16)
    s.node_part[...] = upstream + nt(node_dpre, node_first[0])

    def make(src, dst, sems, index, device):
        return remote(src, dst, sems[0].at[index], sems[1].at[index], device)

    def row_chunk(index):
        return pl.ds(pl.multiple_of(index * 128, 128), 128)

    class Share:
        def __init__(self, owner, first, count, held, final):
            t = SimpleNamespace(**held)
            self.owner, self.first, self.count, self.final = owner, first, count, final
            self.core_in, self.pair = t.core_in, t.pair
            self.a_in, self.a_sum = t.a_in, t.a_sum
            self.b_in, self.b_sum, self.z_in = t.b_in, t.b_sum, t.z_in
            columns_first = owner == 0
            if columns_first:
                self.a_place, self.b_place, a_peers, b_peers = y, x, y_peers, x_peers
                self.cuts = [(slice(None), slice(j * 128, (j + 1) * 128)) for j in range(4)]
            else:
                self.a_place, self.b_place, a_peers, b_peers = x, y, x_peers, y_peers
                self.cuts = [(slice(j * 128, (j + 1) * 128), slice(None)) for j in range(4)]

            def b_cut(k):
                piece = row_chunk((self.b_place + k) % 4)
                return (slice(None), piece, slice(None)) if columns_first else (slice(None), slice(None), piece)

            self.b_own = b_cut(0)
            self.core_copies = [
                make(grads.at[first + m], self.core_in.at[m], t.core_sems, m, partner) for m in range(count)
            ]
            self.a_copies = [
                [
                    make(self.pair.at[(self.a_place + k) % 4, m], self.a_in.at[k - 1, m], t.a_sems, (k - 1, m), a_peers[k])
                    for k in (2, 1, 3)
                ]
                for m in range(count)
            ]
            self.b_copies = [
                make(self.a_sum.at[b_cut(k)], self.b_in.at[k - 1], t.b_sems, k - 1, b_peers[k]) for k in (2, 1, 3)
            ]
            self.z_copies = [
                make(
                    self.b_sum.at[:, pl.ds(pl.multiple_of(((z + k) % ZN) * 16, 16), 16), :],
                    self.z_in.at[k - 1],
                    t.z_sems,
                    k - 1,
                    z_peers[k],
                )
                for k in (4, 3, 5, 2, 6, 1, 7)
            ]
            self.dp_copies = [
                remote(final.at[y], final.at[y], t.dp_sems[0].at[k - 1], t.dp_sems[1].at[y], dp_peers[k])
                for k in range(1, 8)
            ]
            self.dp_in = [
                remote(
                    final.at[(y + k) % YN],
                    final.at[(y + k) % YN],
                    t.dp_sems[0].at[0],
                    t.dp_sems[1].at[(y + k) % YN],
                    dp_peers[1],
                )
                for k in range(YN)
            ]

        def give(self, m):
            @pl.when(core != self.owner)
            def _():
                self.core_copies[m].start()

        def across_a(self, m):
            @pl.when(core == self.owner)
            def _():
                self.core_copies[m].wait_recv()
                for j, (rows, lanes) in enumerate(self.cuts):
                    self.pair[j, m] = (
                        grads[self.first + m, rows, lanes].astype(F32) + self.core_in[m, rows, lanes].astype(F32)
                    ).astype(BF16)
                for copy in self.a_copies[m]:
                    copy.start()

        def across_b(self):
            @pl.when(core == self.owner)
            def _():
                for m in range(self.count):
                    for copy in self.a_copies[m]:
                        copy.wait_recv()
                    self.a_sum[m] = (
                        self.pair[self.a_place, m].astype(F32)
                        + self.a_in[0, m].astype(F32)
                        + self.a_in[1, m].astype(F32)
                        + self.a_in[2, m].astype(F32)
                    ).astype(BF16)
                for copy in self.b_copies:
                    copy.start()

        def across_z(self):
            @pl.when(core == self.owner)
            def _():
                for copy in self.b_copies:
                    copy.wait_recv()
                self.b_sum[...] = (
                    self.a_sum[self.b_own].astype(F32)
                    + self.b_in[0].astype(F32)
                    + self.b_in[1].astype(F32)
                    + self.b_in[2].astype(F32)
                ).astype(BF16)
                for copy in self.z_copies:
                    copy.start()

        def across_dp(self):
            @pl.when(core == self.owner)
            def _():
                for copy in self.z_copies:
                    copy.wait_recv()
                total = self.b_sum[:, pl.ds(pl.multiple_of(z * 16, 16), 16), :].astype(F32)
                for k in range(ZN - 1):
                    total = total + self.z_in[k].astype(F32)
                self.final[y] = total.astype(BF16)
                for copy in self.dp_copies:
                    copy.start()

        def finish(self):
            for k in range(YN):
                if k:
                    self.dp_in[k].wait_recv()
                else:

                    @pl.when(core != self.owner)
                    def _():
                        self.dp_in[0].wait_recv()

        def drain(self):
            @pl.when(core != self.owner)
            def _():
                for copy in self.core_copies:
                    copy.wait_send()

            @pl.when(core == self.owner)
            def _():
                for copies in self.a_copies:
                    for copy in copies:
                        copy.wait_send()
                for copy in self.b_copies + self.z_copies + self.dp_copies:
                    copy.wait_send()

    node_share = Share(1, 4, 3, s.node_share, final_node)
    edge_share = Share(0, 0, 4, s.edge_share, final_edge)
    for m in range(3):
        node_share.give(m)

    dz, dpre = s.dz, s.dpre
    col_scale = jnp.zeros((1, D), F32)
    for i in range(NB):
        rows = slice(i * BM, (i + 1) * BM)
        live = lax.broadcasted_iota(jnp.int32, (BM, 1), 0) + i * BM < live_rows
        message_cot = jnp.where(live, edge_cot[rows, :].astype(F32) + nn(hot[rows, :], aggregate_cot), 0.0)
        hat = normed[rows, :]
        col_scale = col_scale + jnp.sum(message_cot * hat, 0, keepdims=True)
        dz[rows, :] = norm_backward(message_cot, hat, inverse[rows, :], vectors_ref[2:3, :]).astype(BF16)
        if i == 0:
            for m in range(3):
                node_share.across_a(m)
    grads[3] = tn(act[...], dz[...]).astype(BF16)
    edge_share.give(3)
    col_edge = jnp.zeros((1, D), F32)
    received = jnp.zeros((ND, D), F32)
    for i in range(NB):
        rows = slice(i * BM, (i + 1) * BM)
        dpre_b = (nt(dz[rows, :], edge_second[...]) * slope[rows, :]).astype(BF16)
        dpre[rows, :] = dpre_b
        col_edge = col_edge + jnp.sum(dpre_b.astype(F32), 0, keepdims=True)
        received = received + nn(hot_back[:, rows], dpre_b)
        if i == 0:
            edge_share.across_a(3)
    received = received.astype(BF16)
    back = s.back
    back[...] = nn(perm_back[...], dpre[...]).astype(BF16).reshape(GN, SLOTS, D)
    rows_in = s.rows_in
    row_copies = {}
    for j in REDUCE_ORDER:
        target = (z + REDUCE_OFFSET[j] + ZN) % ZN
        row_copies[j] = [
            start(back.at[((x + k) % XN) * ZN + target], rows_in.at[j, x], s.row_sems, (j, k - 1), x_peers[k])
            for k in range(1, XN)
        ]
    grads[2] = tn(h, received).astype(BF16)
    edge_share.give(2)
    grads[0] = tn(edges[...], dpre[...]).astype(BF16)
    edge_share.give(0)
    edge_share.across_a(2)
    edge_share.across_a(0)
    grads[1] = tn(buf[...].reshape(EDGES, D), back[...].reshape(EDGES, D)).astype(BF16)
    edge_share.give(1)

    sums = s.sums
    sums[0] = jnp.concatenate([col_edge, col_node, col_scale, col_node_scale, jnp.zeros((4, D), F32)], axis=0)
    dp_sums = [start(sums.at[0], s.dp_sums.at[k - 1], s.sdp_sems, k - 1, dp_peers[k]) for k in range(1, 8)]
    for j in REDUCE_ORDER:
        target = (z + REDUCE_OFFSET[j] + ZN) % ZN
        rows_in[j, x] = back[x * ZN + target]

    ring_out, ring_in = s.ring_out, s.ring_in
    ring_copies = {}

    def ring_step(j):
        target = (z + REDUCE_OFFSET[j] + ZN) % ZN
        for copy in row_copies[j]:
            copy.wait_recv()
        total = nn(onehot_rows(ND, lists[pl.ds(target, 1), :]), rows_in[j].reshape(ND, D))
        if j:
            for part in range(PARTS):
                piece = slice(part * rows_of, (part + 1) * rows_of)
                partial = total[piece]
                before = j + 1 if j in (2, 1, 6, 5) or (j == 3 and part == 0) else 4 if j == 7 and part == 1 else None
                if before:
                    ring_copies[before, part].wait_recv()
                    partial = partial + ring_in[before, piece].astype(F32)
                ring_out[j, piece] = partial.astype(BF16)
                ring_copies[j, part] = start(
                    ring_out.at[j, piece], ring_in.at[j, piece], s.back_sems, (j, part), up if j < 4 or (j == 4 and part == 0) else down
                )
            return
        for part in range(PARTS):
            ring_copies[1, part].wait_recv()
            ring_copies[5, part].wait_recv()
        total = total + ring_in[1].astype(F32) + ring_in[5].astype(F32)
        node_grad_ref[...] = (
            s.node_part[...] + nt(total.astype(BF16), edge_first[1]) + nt(received, edge_first[2])
        ).astype(BF16)

    def sum_step(parts, source, index):
        total = sums[source]
        for k in range(parts.shape[0]):
            total = total + parts[k]
        sums[index] = total

    edge_grad = s.edge_grad
    for i in range(NB):
        rows = slice(i * BM, (i + 1) * BM)
        edge_grad[rows, :] = (edge_cot[rows, :].astype(F32) + nt(dpre[rows, :], edge_first[0])).astype(BF16)
        if i == 0:
            edge_share.across_a(1)
        ring_step(REDUCE_ORDER[i])
    store_grad = pltpu.make_async_copy(edge_grad, edge_grad_hbm, s.store_sem.at[2])
    store_grad.start()
    ring_step(3)
    node_share.across_b()
    ring_step(6)
    for copy in dp_sums:
        copy.wait_recv()
    sum_step(s.dp_sums, 0, 1)
    x_sums = [start(sums.at[1], s.x_sums.at[k - 1], s.sx_sems, k - 1, x_peers[k]) for k in range(1, XN)]
    node_share.across_z()
    edge_share.across_b()
    ring_step(2)
    ring_step(5)
    node_share.across_dp()
    edge_share.across_z()
    for copy in x_sums:
        copy.wait_recv()
    sum_step(s.x_sums, 1, 2)
    z_sums = [start(sums.at[2], s.z_sums.at[k - 1], s.sz_sems, k - 1, z_peers[k]) for k in range(1, ZN)]
    ring_step(1)
    edge_share.across_dp()
    ring_step(0)
    for copy in z_sums:
        copy.wait_recv()
    sum_step(s.z_sums, 2, 3)
    sums_ref[...] = sums[3]
    store_edges.wait()
    store_nodes.wait()
    store_grad.wait()
    for copy in sent:
        copy.wait_send()
    edge_share.finish()
    node_share.finish()
    node_share.drain()
    edge_share.drain()


def scratch():
    v, dma = pltpu.VMEM, pltpu.SemaphoreType.DMA

    def pair(*size):
        return dma(size), dma(size)

    def share(count, a_shape):
        return dict(
            core_in=v((count, D, D), BF16),
            pair=v((4, count) + a_shape, BF16),
            a_in=v((3, count) + a_shape, BF16),
            a_sum=v((count,) + a_shape, BF16),
            b_in=v((3, count, 128, 128), BF16),
            b_sum=v((count, 128, 128), BF16),
            z_in=v((ZN - 1, count, 16, 128), BF16),
            core_sems=pair(count),
            a_sems=pair(3, count),
            b_sems=pair(3),
            z_sems=pair(ZN - 1),
            dp_sems=(dma((7,)), dma((YN,))),
        )

    return dict(
        edges=v((EDGES, D), BF16),
        edge_first=v((3, D, D), BF16),
        edge_second=v((D, D), BF16),
        node_first=v((2, D, D), BF16),
        node_second=v((D, D), BF16),
        node_cot=v((ND, D), BF16),
        edge_cot=v((EDGES, D), BF16),
        load_sem=dma((11,)),
        node=v((ND, D), BF16),
        senders=v((8, 128), jnp.int32),
        recv=v((8, 128), jnp.int32),
        vectors=v((4, D), F32),
        store_sem=dma((3,)),
        ring=v((ZN, ND, D), BF16),
        stage=v((ZN, XN, SLOTS, D), BF16),
        buf=v((GN, SLOTS, D), BF16),
        lists_own=v((XN, ZN, ND), F32),
        lists_in=v((XN - 1, ZN, ND), F32),
        lists=v((ZN, ND), jnp.int32),
        perm=v((EDGES, EDGES), BF16),
        perm_back=v((EDGES, EDGES), BF16),
        hot=v((EDGES, ND), BF16),
        hot_back=v((ND, EDGES), BF16),
        h_recv=v((ND, D), BF16),
        act=v((EDGES, D), BF16),
        slope=v((EDGES, D), F32),
        normed=v((EDGES, D), F32),
        inverse=v((EDGES, 1), F32),
        new_edges=v((EDGES, D), BF16),
        new_nodes=v((ND, D), BF16),
        edge_grad=v((EDGES, D), BF16),
        node_part=v((ND, D), F32),
        dz=v((EDGES, D), BF16),
        dpre=v((EDGES, D), BF16),
        back=v((GN, SLOTS, D), BF16),
        rows_in=v((ZN, XN, SLOTS, D), BF16),
        ring_out=v((ZN, ND, D), BF16),
        ring_in=v((ZN, ND, D), BF16),
        grads=v((7, D, D), BF16),
        sums=v((4, 8, D), F32),
        dp_sums=v((7, 8, D), F32),
        x_sums=v((XN - 1, 8, D), F32),
        z_sums=v((ZN - 1, 8, D), F32),
        hop_sems=pair(ZN, PARTS),
        list_sems=pair(XN - 1),
        away_sems=pair(ZN, XN - 1),
        row_sems=pair(ZN, XN - 1),
        back_sems=pair(ZN, PARTS),
        sdp_sems=pair(7),
        sx_sems=pair(XN - 1),
        sz_sems=pair(ZN - 1),
        edge_share=share(4, (D, 128)),
        node_share=share(3, (128, D)),
    )


def layer(counts, node, senders, recv, vectors, edges, edge_first, edge_second, node_first, node_second, node_cot, edge_cot):
    vmem = pl.BlockSpec(memory_space=pltpu.VMEM)
    hbm = pl.BlockSpec(memory_space=pl.ANY)
    return pl.pallas_call(
        layer_kernel,
        out_shape=(
            jax.ShapeDtypeStruct((ND, D), BF16),
            jax.ShapeDtypeStruct((EDGES, D), BF16),
            jax.ShapeDtypeStruct((EDGES, D), BF16),
            jax.ShapeDtypeStruct((ND, D), BF16),
            jax.ShapeDtypeStruct((YN, 4, 16, 128), BF16),
            jax.ShapeDtypeStruct((YN, 3, 16, 128), BF16),
            jax.ShapeDtypeStruct((8, D), F32),
        ),
        in_specs=[pl.BlockSpec(memory_space=pltpu.SMEM)] + [hbm] * 11,
        out_specs=(hbm,) * 3 + (vmem,) * 4,
        scratch_shapes=[scratch()],
        compiler_params=pltpu.CompilerParams(
            collective_id=0, has_side_effects=True, vmem_limit_bytes=VMEM_LIMIT
        ),
        name="layer",
    )(counts, node, senders, recv, vectors, edges, edge_first, edge_second, node_first, node_second, node_cot, edge_cot)


def outputs_kernel(*refs):
    copied_in, parts_in, copied_out, small_out = refs[0:4], refs[4:7], refs[7:11], refs[11:16]
    copied, parts, small = refs[16:20], refs[20:23], refs[23:28]
    in_sems, out_sems, part_sems, small_sems = refs[28:32]
    moves = []
    for src, held, dst in zip(copied_in, copied, copied_out):
        size = min(CHUNK, src.shape[0])
        for first in range(0, src.shape[0], size):
            piece, index = pl.ds(first, size), len(moves)
            moves.append(
                (
                    pltpu.make_async_copy(src.at[piece], held.at[piece], in_sems.at[index]),
                    pltpu.make_async_copy(held.at[piece], dst.at[piece], out_sems.at[index]),
                )
            )
    loads = [pltpu.make_async_copy(src, held, part_sems.at[i]) for i, (src, held) in enumerate(zip(parts_in, parts))]
    stores = [pltpu.make_async_copy(held, dst, small_sems.at[i]) for i, (held, dst) in enumerate(zip(small, small_out))]
    for load in loads:
        load.start()
    for fetch, _ in moves:
        fetch.start()
    for load in loads:
        load.wait()
    edge_part, node_part, sums_ref = parts
    edge_first_ref, edge_second_ref, node_first_ref, node_second_ref, vectors_ref = small
    for j in range(YN):
        lanes = slice(j * 128, (j + 1) * 128)
        for m in range(3):
            edge_first_ref[m, :, lanes] = edge_part[j, m].astype(F32)
        edge_second_ref[:, lanes] = edge_part[j, 3].astype(F32)
        for m in range(2):
            node_first_ref[m, :, lanes] = node_part[j, m].astype(F32)
        node_second_ref[:, lanes] = node_part[j, 2].astype(F32)
    shift = (D - lax.axis_index("graph") * 16) % D
    vectors_ref[...] = pltpu.roll(sums_ref[...], shift, 1)[0:4, 0:16]
    for store in stores:
        store.start()
    for fetch, store in moves:
        fetch.wait()
        store.start()
    for _, store in moves:
        store.wait()
    for store in stores:
        store.wait()


def outputs(nodes, edges, edge_grad, node_grad, edge_part, node_part, sums):
    hbm = pl.BlockSpec(memory_space=pl.ANY)
    copied = [((EDGES, D), BF16), ((EDGES, D), BF16), ((ND, D), BF16), ((ND, D), BF16)]
    parts = [((YN, 4, 16, 128), BF16), ((YN, 3, 16, 128), BF16), ((8, D), F32)]
    small = [((3, 16, D), F32), ((16, D), F32), ((2, 16, D), F32), ((16, D), F32), ((4, 16), F32)]
    moves = 2 * EDGES // CHUNK + 2
    new_edges, edge_grad, new_nodes, node_grad, *rest = pl.pallas_call(
        outputs_kernel,
        out_shape=tuple(jax.ShapeDtypeStruct(*one) for one in copied + small),
        in_specs=[hbm] * 7,
        out_specs=(hbm,) * 9,
        scratch_shapes=[pltpu.VMEM(*one) for one in copied + parts + small]
        + [pltpu.SemaphoreType.DMA((count,)) for count in (moves, moves, 3, 5)],
        compiler_params=pltpu.CompilerParams(vmem_limit_bytes=VMEM_LIMIT),
        name="outputs",
    )(edges, edge_grad, nodes, node_grad, edge_part, node_part, sums)
    return new_nodes, new_edges, edge_grad, node_grad, *rest


def body(
    node_latents,
    edge_latents,
    senders,
    receivers,
    block_counts,
    edge_first,
    edge_second,
    node_first,
    node_second,
    vectors,
    node_cotangent,
    edge_cotangent,
):
    new_nodes, new_edges, edge_grad, node_grad, edge_part, node_part, sums = layer(
        block_counts,
        node_latents[0],
        senders,
        receivers,
        vectors,
        edge_latents.reshape(EDGES, D),
        edge_first,
        edge_second,
        node_first,
        node_second,
        node_cotangent[0],
        edge_cotangent.reshape(EDGES, D),
    )
    new_nodes, new_edges, edge_grad, node_grad, grad_ef, grad_es, grad_nf, grad_ns, columns = outputs(
        new_nodes, new_edges, edge_grad, node_grad, edge_part, node_part, sums
    )
    shape = edge_latents.shape
    return (
        new_nodes[None],
        new_edges.reshape(shape),
        node_grad[None],
        edge_grad.reshape(shape),
        grad_ef,
        grad_es,
        grad_nf,
        grad_ns,
        columns,
    )


def solution(mesh):
    return jax.shard_map(
        body,
        mesh=mesh,
        in_specs=(
            P("dp", "graph", None),
            P("dp", "graph", None, None),
            P("graph", None),
            P("graph", None),
            P("graph"),
            P(),
            P(),
            P(),
            P(),
            P(),
            P("dp", "graph", None),
            P("dp", "graph", None, None),
        ),
        out_specs=(
            P("dp", "graph", None),
            P("dp", "graph", None, None),
            P("dp", "graph", None),
            P("dp", "graph", None, None),
            P(None, "graph", None),
            P("graph", None),
            P(None, "graph", None),
            P("graph", None),
            P(None, "graph"),
        ),
        check_vma=False,
    )
```
